128 devices in a mesh: dp: 16 (over z_lo, y, core), col: 8 (over x, z_hi).
Axes of the slice: x: 4, y: 4, z: 4 (z_hi: 2, z_lo: 2; z = z_hi * 2 + z_lo), core: 2. Of those that a mesh axis runs over, the one named last changes fastest.
Arguments:
- image_emb: bfloat16 [8192, 1024], P(('dp', 'col')), may hold values from -4 to 4
- text_emb: bfloat16 [8192, 1024], P(('col', 'dp')), may hold values from -4 to 4
- pairs: int32 [8192], P('dp'), may hold values from 0 to 8191, as said below
- logit_scale: float32 [1], replicated, may hold values from 10 to 400
- tokens: bfloat16 [128, 257, 1408], P(('dp', 'col')), may hold values from -6 to 6
- norm_gain: float32 [1408], replicated, may hold values from 0.1 to 1.9
- w_in: bfloat16 [1408, 6144], P('dp', 'col'), may hold values from -0.15625 to 0.15625
- w_out: bfloat16 [6144, 1408], P('col', 'dp'), may hold values from -0.078125 to 0.078125
- proj: bfloat16 [1408, 1024], P('dp'), may hold values from -0.15625 to 0.15625
Outputs:
- image_grad: float32 [8192, 1024], P(('dp', 'col'))
- text_grad: float32 [8192, 1024], P(('col', 'dp'))
- grad_w_in: float32 [1408, 6144], P('dp', 'col')
- grad_w_out: float32 [6144, 1408], P('col', 'dp')
- grad_proj: float32 [1408, 1024], P('dp')
The draws below stay inside these ranges and needn't reach their ends.
Inputs may be any that keep to these rules, and one draw needn't show every extreme that they name: `pairs`: a permutation of 0 to 8191.
All inputs are finite; a program needn't handle non-finite values.
Results may differ from the reference program's by a relative error of at most 0.0075.
The reference program's roundings to bfloat16 on the way (of `dlogit`, `grad_low`, `normed`, `act_mean`, `pool_low`, `dpool_low` and `pre_grad`) count: a program that leaves them out, or rounds other values in their place, can miss the bound.
Values may be sent and summed in bfloat16 or wider, within the bound.
No kernel may reach another device: no remote copies, remote signals or barrier semaphores. Data moves between devices by JAX's collectives and lax.ppermute only.
A program may use at most 128 MiB of HBM per device.

```python
import jax
import jax.numpy as jnp
from jax import lax

D = 1408
FF = 6144
EMB = 1024
SEQ = 257
IMG_DP = 512
IMG_DEV = 1
BATCH = 8192
ENC_IMGS = 128
N_COL = 8
DEVICES = 128


def shared_rows(key):
    order = jax.random.permutation(jax.random.fold_in(key, 101), BATCH).astype(jnp.int32)
    common = jax.random.normal(jax.random.fold_in(key, 102), (BATCH, EMB), jnp.float32)
    nearby = jax.random.normal(jax.random.fold_in(key, 103), (BATCH, EMB), jnp.float32)
    return (order, common, nearby)


def paired_rows(key, common, nearby, weight_low, weight_high, exact_share, scale_low, scale_high):
    row_ids = jnp.arange(BATCH)
    twins = jnp.where((row_ids % 64 == 1)[:, None], jnp.roll(common, 1, axis=0) + 0.1 * nearby, common)
    weights = jax.random.uniform(jax.random.fold_in(key, 7), (BATCH, 1), jnp.float32, weight_low, weight_high)
    noise = jax.random.normal(jax.random.fold_in(key, 8), (BATCH, EMB), jnp.float32)
    mixed = weights * twins + noise
    exact = (row_ids % 64 < 2)[:, None] & (exact_share > 0)
    mixed = jnp.where(exact, twins, mixed)
    row_scale = jnp.exp(jax.random.uniform(jax.random.fold_in(key, 9), (BATCH, 1), jnp.float32, jnp.log(scale_low), jnp.log(scale_high)))
    return jnp.clip(mixed * row_scale * 0.03125, -4.0, 4.0)


def draw_image_emb(key, part):
    order, common, nearby = shared_rows(key)
    key = jax.random.fold_in(key, 1)
    return paired_rows(key, common, nearby, 1.0, 1.0, 0, 0.5, 2.0).astype(jnp.bfloat16)


def draw_text_emb(key, part):
    order, common, nearby = shared_rows(key)
    key = jax.random.fold_in(key, 2)
    placed = paired_rows(key, common, nearby, 1.0, 1.0, 0, 0.5, 2.0)
    return jnp.zeros((BATCH, EMB), jnp.float32).at[order].set(placed).astype(jnp.bfloat16)


def draw_pairs(key, part):
    order, common, nearby = shared_rows(key)
    return order


def draw_logit_scale(key, part):
    key = jax.random.fold_in(key, 4)
    return jnp.exp(jax.random.uniform(key, (1,), jnp.float32, jnp.log(10.0), jnp.log(50.0)))


def level_of(rng, dims, pieces, least, high):
    def one(position, blocks):
        heights = jax.random.uniform(jax.random.fold_in(jax.random.fold_in(rng, 6), position), (blocks,), jnp.float32, least / len(pieces), high / len(pieces))
        return jnp.repeat(jnp.exp(heights), dims[position] // blocks).reshape((-1,) + (1,) * (len(dims) - position - 1))

    factor_of = one(*pieces[0])
    for cut in pieces[1:]:
        factor_of = factor_of * one(*cut)
    return factor_of


def scatter_about(key, dims, width, most, cuts=(), kind=jnp.bfloat16):
    array = jax.random.normal(key, dims, jnp.float32) * width
    if len(cuts) > 0:
        array = level_of(key, dims, cuts, -0.22, 0.18) * array
    return jnp.clip(array, min=-most, max=most).astype(kind)


def setup_inputs(seed: int = 0) -> dict:
    seeds = jax.random.split(jax.random.key(seed), 10)
    return {
        "image_emb": draw_image_emb(jax.random.fold_in(seeds[9], 71), 0),
        "text_emb": draw_text_emb(jax.random.fold_in(seeds[9], 71), 0),
        "pairs": draw_pairs(jax.random.fold_in(seeds[9], 71), 0),
        "logit_scale": draw_logit_scale(jax.random.fold_in(seeds[9], 71), 0),
        "tokens": scatter_about(seeds[4], (ENC_IMGS, SEQ, D), 1.0, 6.0, ((0, 128),)),
        "norm_gain": jnp.clip(1.0 + 0.18 * jax.random.normal(seeds[5], (D,), jnp.float32), 0.1, 1.9),
        "w_in": scatter_about(seeds[6], (D, FF), D ** -0.5, 0.15625, ((0, 16), (1, 8))),
        "w_out": scatter_about(seeds[7], (FF, D), FF ** -0.5, 0.078125, ((0, 8), (1, 16))),
        "proj": scatter_about(seeds[8], (D, EMB), D ** -0.5, 0.15625, ((0, 16),)),
    }


epsilon = 1e-06
inv_root_two_pi = 0.3989422804014327

def unit_rows(raw):
    values = raw.astype(jnp.float32)
    inverse = lax.rsqrt(lax.optimization_barrier(jnp.sum(values * values, axis=1, keepdims=True)) + epsilon)
    return (values * inverse, inverse)

def gelu_slope(pre_act):
    return 0.5 * (1.0 + jax.scipy.special.erf(pre_act * 0.7071067811865476)) + pre_act * jnp.exp(-0.5 * pre_act * pre_act) * inv_root_two_pi

def contract_rows(left, right):
    return lax.dot_general(left, right, (((0,), (0,)), ((), ())), preferred_element_type=jnp.float32)

def contract_cols(left, right):
    return lax.dot_general(left, right, (((1,), (1,)), ((), ())), preferred_element_type=jnp.float32)

def reference(image_emb, text_emb, pairs, logit_scale, tokens, norm_gain, w_in, w_out, proj):
    img_unit, img_inv = unit_rows(image_emb)
    txt_unit, txt_inv = unit_rows(text_emb)
    img_low = img_unit.astype(jnp.bfloat16)
    txt_low = txt_unit.astype(jnp.bfloat16)
    temper = logit_scale[0]
    block_count = BATCH // IMG_DP
    column_ids = jnp.arange(BATCH, dtype=jnp.int32)

    def block_logits(block_idx):
        begin = (block_idx * IMG_DP).astype(jnp.int32)
        rows_low = lax.dynamic_slice_in_dim(img_low, begin, IMG_DP, 0)
        row_pairs = lax.dynamic_slice_in_dim(pairs, begin, IMG_DP, 0)
        logits = temper * contract_cols(rows_low, txt_low)
        matches = (row_pairs[:, None] == column_ids[None, :]).astype(logits.dtype)
        return (rows_low, logits, matches)

    def first_pass(running, block_idx):
        col_top, col_mass = running
        rows_low, logits, matches = block_logits(block_idx)
        row_top = lax.optimization_barrier(jnp.max(logits, axis=1))
        row_lse = row_top + jnp.log(lax.optimization_barrier(jnp.sum(jnp.exp(logits - row_top[:, None]), axis=1)))
        new_top = jnp.maximum(col_top, lax.optimization_barrier(jnp.max(logits, axis=0)))
        col_mass = col_mass * jnp.exp(col_top - new_top) + lax.optimization_barrier(jnp.sum(jnp.exp(logits - new_top[None, :]), axis=0))
        return ((new_top, col_mass), row_lse)
    start = (jnp.full((BATCH,), -1e+30, dtype=jnp.float32), jnp.zeros((BATCH,), jnp.float32))
    block_ids = jnp.arange(block_count, dtype=jnp.int32)
    (col_top, col_mass), row_lse = lax.scan(first_pass, start, block_ids)
    row_lse = row_lse.reshape(BATCH)
    col_lse = col_top + jnp.log(col_mass)

    def second_pass(txt_acc, block_idx):
        rows_low, logits, matches = block_logits(block_idx)
        begin = (block_idx * IMG_DP).astype(jnp.int32)
        lse_rows = lax.dynamic_slice_in_dim(row_lse, begin, IMG_DP, 0)
        dlogit = (0.5 * (jnp.exp(logits - lse_rows[:, None]) + jnp.exp(logits - col_lse[None, :])) - matches).astype(jnp.bfloat16)
        img_block = jnp.dot(dlogit, txt_low, preferred_element_type=jnp.float32)
        return (txt_acc + contract_rows(dlogit, rows_low), img_block)
    txt_acc, img_blocks = lax.scan(second_pass, jnp.zeros((BATCH, EMB), jnp.float32), block_ids)
    img_dir = temper * img_blocks.reshape(BATCH, EMB)
    txt_dir = temper * txt_acc
    image_grad = img_inv * (img_dir - img_unit * lax.optimization_barrier(jnp.sum(img_unit * img_dir, axis=1, keepdims=True)))
    text_grad = txt_inv * (txt_dir - txt_unit * lax.optimization_barrier(jnp.sum(txt_unit * txt_dir, axis=1, keepdims=True)))
    rows_dev = IMG_DP // N_COL
    cached = image_grad.reshape(DEVICES, rows_dev, EMB)[:, :IMG_DEV].reshape(ENC_IMGS, EMB)

    def encode(image):
        floats = image.astype(jnp.float32)
        center = lax.optimization_barrier(jnp.mean(floats, axis=1, keepdims=True))
        spread = lax.optimization_barrier(jnp.mean(jnp.square(floats - center), axis=1, keepdims=True))
        normed = ((floats - center) * lax.rsqrt(spread + epsilon) * norm_gain).astype(jnp.bfloat16)
        pre_act = jnp.dot(normed, w_in, preferred_element_type=jnp.float32)
        return (normed, pre_act)

    def image_stats(image):
        normed, pre_act = encode(image)
        return (lax.optimization_barrier(jnp.mean(jax.nn.gelu(pre_act, approximate=False), axis=0)), lax.optimization_barrier(jnp.mean(image.astype(jnp.float32), axis=0)))
    act_mean, token_mean = lax.map(image_stats, tokens)
    act_low = act_mean.astype(jnp.bfloat16)
    pooled = token_mean + jnp.dot(act_low, w_out, preferred_element_type=jnp.float32)
    pool_low = pooled.astype(jnp.bfloat16)
    grad_low = cached.astype(jnp.bfloat16)
    dpool_low = contract_cols(grad_low, proj).astype(jnp.bfloat16)
    act_grad = contract_cols(dpool_low, w_out) / SEQ

    def accumulate(total, item):
        image, image_slope = item
        normed, pre_act = encode(image)
        pre_grad = (gelu_slope(pre_act) * image_slope[None, :]).astype(jnp.bfloat16)
        return (total + contract_rows(normed, pre_grad), jnp.zeros((), jnp.float32))
    grad_w_in, unused = lax.scan(accumulate, jnp.zeros((D, FF), jnp.float32), (tokens, act_grad))
    grad_w_out = contract_rows(act_low, dpool_low)
    grad_proj = contract_rows(pool_low, grad_low)
    return (image_grad, text_grad, grad_w_in, grad_w_out, grad_proj)
```

```python
import functools

import jax
import jax.numpy as jnp
from jax import lax
from jax.experimental import pallas as pl
from jax.experimental.pallas import tpu as pltpu
from jax.sharding import PartitionSpec as P

epsilon = 1e-06
inv_root_two_pi = 0.3989422804014327
root_half = 0.7071067811865476
bf16 = jnp.bfloat16
f32 = jnp.float32


def unit_rows(raw):
    values = raw.astype(f32)
    inverse = lax.rsqrt(jnp.sum(values * values, axis=-1, keepdims=True) + epsilon)
    return (values * inverse, inverse)


def contract_rows(left, right):
    return lax.dot_general(left, right, (((0,), (0,)), ((), ())), preferred_element_type=f32)


def contract_cols(left, right):
    return lax.dot_general(left, right, (((1,), (1,)), ((), ())), preferred_element_type=f32)


def share(piece, axis):
    count = lax.axis_size(axis)
    return lax.all_to_all(
        jnp.broadcast_to(piece[None], (count,) + piece.shape), axis, 0, 0, tiled=True
    )


def forward_kernel(tok_ref, gain_ref, win_ref, normed_ref, slope_ref, act_ref, mean_ref):
    floats = tok_ref[0].astype(f32)
    seq = floats.shape[0]
    center = jnp.mean(floats, axis=1, keepdims=True)
    shifted = floats - center
    spread = jnp.mean(shifted * shifted, axis=1, keepdims=True)
    normed = (shifted * lax.rsqrt(spread + epsilon) * gain_ref[...]).astype(bf16)
    normed_ref[0] = normed
    mean_ref[0] = jnp.sum(floats, axis=0, keepdims=True) * (1.0 / seq)
    pre = jnp.dot(normed, win_ref[...], preferred_element_type=f32)
    half = 0.5 * (1.0 + lax.erf(pre * root_half))
    act_ref[0] = jnp.sum(pre * half, axis=0, keepdims=True) * (1.0 / seq)
    slope_ref[0] = half + pre * jnp.exp(-0.5 * pre * pre) * inv_root_two_pi


def encode(tokens, gain, weights, hidden):
    images, seq, width = tokens.shape
    return pl.pallas_call(
        forward_kernel,
        grid=(images,),
        in_specs=[
            pl.BlockSpec((1, seq, width), lambda i: (i, 0, 0)),
            pl.BlockSpec((1, width), lambda i: (0, 0)),
            pl.BlockSpec((width, hidden), lambda i: (0, 0)),
        ],
        out_specs=[
            pl.BlockSpec((1, seq, width), lambda i: (i, 0, 0)),
            pl.BlockSpec((1, seq, hidden), lambda i: (i, 0, 0)),
            pl.BlockSpec((1, 1, hidden), lambda i: (i, 0, 0)),
            pl.BlockSpec((1, 1, width), lambda i: (i, 0, 0)),
        ],
        out_shape=[
            jax.ShapeDtypeStruct((images, seq, width), bf16),
            jax.ShapeDtypeStruct((images, seq, hidden), f32),
            jax.ShapeDtypeStruct((images, 1, hidden), f32),
            jax.ShapeDtypeStruct((images, 1, width), f32),
        ],
        compiler_params=pltpu.CompilerParams(vmem_limit_bytes=48 * 2**20),
        cost_estimate=pl.CostEstimate(
            flops=2 * images * seq * width * hidden,
            bytes_accessed=images * seq * (4 * width + 4 * hidden),
            transcendentals=images * seq * hidden * 2,
        ),
        name="encode",
    )(tokens, gain, weights)


def backward_kernel(core_ref, normed_ref, slope_ref, grad_ref, keep_ref, send_ref, total):
    step = pl.program_id(0)
    pre_grad = (slope_ref[0] * grad_ref[0]).astype(bf16)
    term = contract_rows(normed_ref[0], pre_grad)

    @pl.when(step == 0)
    def _():
        total[...] = term

    @pl.when(step > 0)
    def _():
        total[...] += term

    @pl.when(step == pl.num_programs(0) - 1)
    def _():
        core = core_ref[0]
        pairs, rows, _ = keep_ref.shape
        for pair in range(pairs):
            mine = pl.multiple_of((2 * pair + core) * rows, 8)
            other = pl.multiple_of((2 * pair + 1 - core) * rows, 8)
            keep_ref[pair] = total[pl.ds(mine, rows), :]
            send_ref[pair] = total[pl.ds(other, rows), :].astype(bf16)


def weigh(core, normed, slope, act_grad, rows):
    images, seq, width = normed.shape
    hidden = slope.shape[2]
    pairs = width // rows // 2
    return pl.pallas_call(
        backward_kernel,
        grid=(images,),
        in_specs=[
            pl.BlockSpec(memory_space=pltpu.SMEM),
            pl.BlockSpec((1, seq, width), lambda i: (i, 0, 0)),
            pl.BlockSpec((1, seq, hidden), lambda i: (i, 0, 0)),
            pl.BlockSpec((1, 1, hidden), lambda i: (i, 0, 0)),
        ],
        out_specs=[
            pl.BlockSpec((pairs, rows, hidden), lambda i: (0, 0, 0)),
            pl.BlockSpec((pairs, rows, hidden), lambda i: (0, 0, 0)),
        ],
        out_shape=[
            jax.ShapeDtypeStruct((pairs, rows, hidden), f32),
            jax.ShapeDtypeStruct((pairs, rows, hidden), bf16),
        ],
        scratch_shapes=[pltpu.VMEM((width, hidden), f32)],
        compiler_params=pltpu.CompilerParams(vmem_limit_bytes=48 * 2**20),
        cost_estimate=pl.CostEstimate(
            flops=2 * images * seq * width * hidden,
            bytes_accessed=images * seq * (2 * width + 4 * hidden),
            transcendentals=0,
        ),
        name="weigh",
    )(core, normed, slope, act_grad)


def project(partial, unit):
    return partial - unit * jnp.sum(unit * partial, axis=1, keepdims=True)


def on_device(image_emb, text_emb, pairs, logit_scale, tokens, norm_gain, w_in, w_out, proj):
    dp_size = lax.axis_size("dp")
    hidden = w_in.shape[1]
    rows_d = w_in.shape[0]
    _, seq, width = tokens.shape
    temper = logit_scale[0]

    all_img = share(image_emb, "col")
    all_txt = share(text_emb, "dp")
    all_tok = share(tokens[0], "col")
    weights = lax.all_gather(
        jnp.concatenate((w_in, w_out.T, proj), axis=1), "dp", axis=0, tiled=True
    )

    own_rows = image_emb.shape[0]
    groups = all_img.shape[0]
    img_unit, img_inv = unit_rows(all_img.reshape(-1, image_emb.shape[1]))
    txt_unit, txt_inv = unit_rows(all_txt.reshape(-1, image_emb.shape[1]))
    img_low = img_unit.astype(bf16)
    txt_low = txt_unit.astype(bf16)
    logits = temper * contract_cols(img_low, txt_low)
    txt_count = txt_low.shape[0]
    col_base = lax.axis_index("col") * txt_count
    matches = (
        pairs[:, None] == col_base + jnp.arange(txt_count, dtype=jnp.int32)[None, :]
    ).astype(f32)
    row_top = jnp.max(logits, axis=1)
    row_mass = jnp.sum(jnp.exp(logits - row_top[:, None]), axis=1)
    col_top = jnp.max(logits, axis=0)
    col_mass = jnp.sum(jnp.exp(logits - col_top[None, :]), axis=0)
    row_stats = share(jnp.stack((row_top, row_mass)), "col")
    col_stats = share(jnp.stack((col_top, col_mass)), "dp")

    def lse(stats):
        peak = jnp.max(stats[:, 0], axis=0)
        return peak + jnp.log(jnp.sum(stats[:, 1] * jnp.exp(stats[:, 0] - peak), axis=0))

    row_lse = lse(row_stats)
    col_lse = lse(col_stats)
    dlogit = (
        0.5 * (jnp.exp(logits - row_lse[:, None]) + jnp.exp(logits - col_lse[None, :])) - matches
    ).astype(bf16)

    cached_part = jnp.dot(
        dlogit.reshape(groups, own_rows, txt_count)[:, 0], txt_low, preferred_element_type=f32
    )
    cached_dir = temper * jnp.sum(share(cached_part, "col"), axis=0)
    cached_unit, cached_inv = unit_rows(all_img[:, 0])
    grad_low = (cached_inv * project(cached_dir, cached_unit)).astype(bf16)

    img_part = project(jnp.dot(dlogit, txt_low, preferred_element_type=f32), img_unit)
    img_sum = lax.all_to_all(
        img_part.astype(bf16).reshape(groups, own_rows, -1), "col", 0, 0, tiled=True
    )
    txt_part = project(contract_rows(dlogit, img_low), txt_unit)
    txt_sum = lax.all_to_all(
        txt_part.astype(bf16).reshape(dp_size, own_rows, -1), "dp", 0, 0, tiled=True
    )
    _, own_img_inv = unit_rows(image_emb)
    _, own_txt_inv = unit_rows(text_emb)
    image_grad = own_img_inv * temper * jnp.sum(img_sum.astype(f32), axis=0)
    text_grad = own_txt_inv * temper * jnp.sum(txt_sum.astype(f32), axis=0)

    normed, slope, act_mean, token_mean = encode(all_tok, norm_gain[None, :], weights, hidden)
    act_low = act_mean[:, 0].astype(bf16)
    out_t = weights[:, hidden : 2 * hidden]
    pool_part = contract_cols(act_low, out_t)
    pooled = token_mean[:, 0] + jnp.sum(share(pool_part, "col"), axis=0)
    pool_low = pooled.astype(bf16)
    dpool_low = contract_cols(grad_low, weights[:, 2 * hidden :]).astype(bf16)
    act_grad = jnp.dot(dpool_low, out_t, preferred_element_type=f32) / seq
    core = lax.rem(lax.axis_index("dp"), 2).astype(jnp.int32)[None]
    keep, send = weigh(core, normed, slope, act_grad[:, None, :], rows_d)
    swap = [(i, i ^ 1) for i in range(dp_size)]
    chip_sum = (keep + lax.ppermute(send, "dp", swap).astype(f32)).astype(bf16)
    chips = [list(range(0, dp_size, 2)), list(range(1, dp_size, 2))]
    in_sum = lax.all_to_all(chip_sum, "dp", 0, 0, axis_index_groups=chips, tiled=True)
    grad_w_in = jnp.sum(in_sum.astype(f32), axis=0)

    def slices(array):
        return array.reshape(-1, dp_size, rows_d).transpose(1, 0, 2)

    mixed = jnp.concatenate(
        (
            jnp.broadcast_to(act_low[None], (dp_size,) + act_low.shape),
            jnp.broadcast_to(grad_low[None], (dp_size,) + grad_low.shape),
            slices(dpool_low),
            slices(pool_low),
        ),
        axis=2,
    )
    mixed = lax.all_to_all(mixed, "dp", 0, 0, tiled=True)
    mixed = mixed.reshape(-1, mixed.shape[2])
    emb = grad_low.shape[1]
    act_all = mixed[:, :hidden]
    low_all = mixed[:, hidden : hidden + emb]
    dpool_all = mixed[:, hidden + emb : hidden + emb + rows_d]
    pool_all = mixed[:, hidden + emb + rows_d :]
    grad_w_out = contract_rows(act_all, dpool_all)
    grad_proj = contract_rows(pool_all, low_all)
    return (image_grad, text_grad, grad_w_in, grad_w_out, grad_proj)


def solution(mesh):
    in_specs = (
        P(("dp", "col"), None),
        P(("col", "dp"), None),
        P("dp"),
        P(),
        P(("dp", "col"), None, None),
        P(),
        P("dp", "col"),
        P("col", "dp"),
        P("dp", None),
    )
    out_specs = (
        P(("dp", "col"), None),
        P(("col", "dp"), None),
        P("dp", "col"),
        P("col", "dp"),
        P("dp", None),
    )
    return jax.shard_map(
        on_device, mesh=mesh, in_specs=in_specs, out_specs=out_specs, check_vma=False
    )
```

```python
import functools

import jax
import jax.numpy as jnp
from jax import lax
from jax.experimental import pallas as pl
from jax.experimental.pallas import tpu as pltpu
from jax.sharding import PartitionSpec as P

epsilon = 1e-06
inv_root_two_pi = 0.3989422804014327
root_half = 0.7071067811865476
bf16 = jnp.bfloat16
f32 = jnp.float32


def unit_rows(raw):
    values = raw.astype(f32)
    inverse = lax.rsqrt(jnp.sum(values * values, axis=-1, keepdims=True) + epsilon)
    return (values * inverse, inverse)


def contract_rows(left, right):
    return lax.dot_general(left, right, (((0,), (0,)), ((), ())), preferred_element_type=f32)


def contract_cols(left, right):
    return lax.dot_general(left, right, (((1,), (1,)), ((), ())), preferred_element_type=f32)


def share(piece, axis, groups=None):
    count = len(groups[0]) if groups else lax.axis_size(axis)
    copies = jnp.broadcast_to(piece[None], (count,) + piece.shape)
    return lax.all_to_all(copies, axis, 0, 0, axis_index_groups=groups, tiled=True)


def encode_kernel(cuts, *refs):
    images = len(cuts)
    pieces = 1 + max(cut[0] for image in cuts for cut in image)
    toks, refs = refs[:pieces], refs[pieces:]
    gain_ref, win_ref, main_ref, last_ref, slope_ref, slope_last_ref, act_ref, slots, sems = refs
    step = pl.program_id(0)

    def copies(index):
        slot = index % 2
        return [
            pltpu.make_async_copy(
                toks[piece], slots.at[slot, :, pl.ds(start, size)], sems.at[slot, k]
            )
            for k, (piece, start, size) in enumerate(cuts[index])
        ]

    def each(index, act):
        for k in range(images):

            @pl.when(index == k)
            def _():
                for copy in copies(k):
                    act(copy)

    @pl.when(step == 0)
    def _():
        each(step, lambda copy: copy.start())

    @pl.when(step + 1 < images)
    def _():
        each(step + 1, lambda copy: copy.start())

    each(step, lambda copy: copy.wait())
    slot = lax.rem(step, 2)
    floats = slots[slot].astype(f32)
    seq = floats.shape[0]
    center = jnp.mean(floats, axis=1, keepdims=True)
    shifted = floats - center
    spread = jnp.mean(shifted * shifted, axis=1, keepdims=True)
    wide = shifted * lax.rsqrt(spread + epsilon) * gain_ref[...]
    normed = wide.astype(bf16)
    main_ref[...] = normed[: seq - 1].T
    last_ref[0] = normed[seq - 1 :]
    pre = jnp.dot(normed, win_ref[...], preferred_element_type=f32)
    half = 0.5 * (1.0 + lax.erf(pre * root_half))
    act_ref[0] = jnp.sum(pre * half, axis=0, keepdims=True) * (1.0 / seq)
    slope = half + pre * jnp.exp(-0.5 * pre * pre) * inv_root_two_pi
    slope_ref[0] = slope[: seq - 1]
    slope_last_ref[0] = slope[seq - 1 :]


def encode(tokens, gain, weights, hidden):
    seq, width = tokens[0][0].shape[0], sum(piece.shape[1] for piece in tokens[0])
    images = len(tokens)
    pieces, cuts = [], []
    for image in tokens:
        ends = [sum(piece.shape[1] for piece in image[:k]) for k in range(len(image))]
        cuts.append(
            [(len(pieces) + k, end, piece.shape[1]) for k, (end, piece) in enumerate(zip(ends, image))]
        )
        pieces += image
    return pl.pallas_call(
        functools.partial(encode_kernel, cuts),
        grid=(images,),
        in_specs=[pl.BlockSpec(memory_space=pltpu.HBM)] * len(pieces)
        + [
            pl.BlockSpec((1, width), lambda i: (0, 0)),
            pl.BlockSpec((width, hidden), lambda i: (0, 0)),
        ],
        out_specs=[
            pl.BlockSpec((width, seq - 1), lambda i: (0, i)),
            pl.BlockSpec((1, 1, width), lambda i: (i, 0, 0)),
            pl.BlockSpec((1, seq - 1, hidden), lambda i: (i, 0, 0)),
            pl.BlockSpec((1, 1, hidden), lambda i: (i, 0, 0)),
            pl.BlockSpec((1, 1, hidden), lambda i: (i, 0, 0)),
        ],
        out_shape=[
            jax.ShapeDtypeStruct((width, images * (seq - 1)), bf16),
            jax.ShapeDtypeStruct((images, 1, width), bf16),
            jax.ShapeDtypeStruct((images, seq - 1, hidden), f32),
            jax.ShapeDtypeStruct((images, 1, hidden), f32),
            jax.ShapeDtypeStruct((images, 1, hidden), f32),
        ],
        scratch_shapes=[
            pltpu.VMEM((2, seq, width), bf16),
            pltpu.SemaphoreType.DMA((2, 2)),
        ],
        compiler_params=pltpu.CompilerParams(vmem_limit_bytes=60 * 2**20),
        cost_estimate=pl.CostEstimate(
            flops=2 * images * seq * width * hidden,
            bytes_accessed=images * seq * (4 * width + 4 * hidden),
            transcendentals=images * seq * hidden * 2,
        ),
        name="encode",
    )(*pieces, gain, weights)


def weigh_kernel(core_ref, order_ref, *refs):
    grad_ref, keep_ref, send_ref, pre_grad, pre_last, last_rows, last_term, total = refs[-8:]
    sets = (refs[0:4], refs[4:8])
    images, tokens, _ = sets[0][2].shape

    @pl.when(pl.program_id(0) == 0)
    def _():
        for k, (_, last_ref, slope_ref, slope_last_ref) in enumerate(sets):
            for i in range(images):
                row = grad_ref[order_ref[k * images + i]]
                pre_grad[k, pl.ds(i * tokens, tokens), :] = (slope_ref[i] * row).astype(bf16)
                pre_last[pl.ds(k * images + i, 1), :] = slope_last_ref[i] * row
                last_rows[pl.ds(k * images + i, 1), :] = last_ref[i].astype(f32)
        last_term[...] = contract_rows(last_rows[...].astype(bf16), pre_last[...].astype(bf16))

    chunk = total.shape[0]
    value = last_term[pl.ds(pl.multiple_of(pl.program_id(0) * chunk, 8), chunk), :]
    for k, (main_ref, _, _, _) in enumerate(sets):
        value += jnp.dot(main_ref[...], pre_grad[k], preferred_element_type=f32)
    total[...] = value
    core = core_ref[0]
    pairs, rows, _ = keep_ref.shape
    for pair in range(pairs):
        mine = pl.multiple_of((2 * pair + core) * rows, 8)
        other = pl.multiple_of((2 * pair + 1 - core) * rows, 8)
        keep_ref[pair] = total[pl.ds(mine, rows), :]
        send_ref[pair] = total[pl.ds(other, rows), :].astype(bf16)


def weigh(core, order, sets, act_grad, rows):
    main, _, slope, _ = sets[0]
    images, tokens, hidden = slope.shape
    width = main.shape[0]
    chunk = 4 * rows
    steps = width // chunk
    set_specs = [
        pl.BlockSpec((chunk, images * tokens), lambda i: (i, 0)),
        pl.BlockSpec((images, 1, width), lambda i: (0, 0, 0)),
        pl.BlockSpec((images, tokens, hidden), lambda i: (0, 0, 0)),
        pl.BlockSpec((images, 1, hidden), lambda i: (0, 0, 0)),
    ]
    operands = []
    for main, last, slope, slope_last in sets:
        operands += [main, last, slope, slope_last]
    return pl.pallas_call(
        weigh_kernel,
        grid=(steps,),
        in_specs=[pl.BlockSpec(memory_space=pltpu.SMEM)] * 2
        + set_specs * len(sets)
        + [pl.BlockSpec(act_grad.shape, lambda i: (0, 0, 0))],
        out_specs=[
            pl.BlockSpec((2, rows, hidden), lambda i: (i, 0, 0)),
            pl.BlockSpec((2, rows, hidden), lambda i: (i, 0, 0)),
        ],
        out_shape=[
            jax.ShapeDtypeStruct((2 * steps, rows, hidden), f32),
            jax.ShapeDtypeStruct((2 * steps, rows, hidden), bf16),
        ],
        scratch_shapes=[
            pltpu.VMEM((len(sets), images * tokens, hidden), bf16),
            pltpu.VMEM((len(sets) * images, hidden), f32),
            pltpu.VMEM((len(sets) * images, width), f32),
            pltpu.VMEM((width, hidden), f32),
            pltpu.VMEM((chunk, hidden), f32),
        ],
        compiler_params=pltpu.CompilerParams(vmem_limit_bytes=60 * 2**20),
        cost_estimate=pl.CostEstimate(
            flops=4 * images * tokens * width * hidden,
            bytes_accessed=2 * images * tokens * (2 * width + 4 * hidden),
            transcendentals=0,
        ),
        name="weigh",
    )(core, order, *operands, act_grad)


def unit_kernel(where_ref, *refs):
    pieces = refs[:-10]
    txt_hbm, raw_img, low_img, low_txt, inv_img, inv_txt, first_rows, halves, raw_txt, sems = refs[-10:]
    blocks = raw_txt.shape[0]
    part = blocks // len(pieces)
    img_loads, txt_loads = [], []
    for hop, piece in enumerate(pieces):
        chunk = pl.ds(hop * part, part)
        img_loads.append(pltpu.make_async_copy(piece, halves.at[hop], sems.at[0, hop]))
        txt_loads.append(
            pltpu.make_async_copy(txt_hbm.at[chunk], raw_txt.at[chunk], sems.at[1, hop])
        )
    for load in img_loads + txt_loads:
        load.start()
    for hop, load in enumerate(img_loads):
        load.wait()
        for flag in range(2):
            spot = where_ref[2 * hop + flag]
            values = halves[hop, flag]
            unit, inverse = unit_rows(values)
            raw_img[spot] = values
            first_rows[pl.ds(spot, 1), :] = values[0:1].astype(f32)
            low_img[spot] = unit.astype(bf16)
            inv_img[spot] = inverse
    for hop, load in enumerate(txt_loads):
        load.wait()
        for k in range(hop * part, hop * part + part):
            unit, inverse = unit_rows(raw_txt[k])
            low_txt[k] = unit.astype(bf16)
            inv_txt[k] = inverse


def gather_units(where, ring_img, raw_txt):
    texts, rows, width = raw_txt.shape
    images = 2 * len(ring_img)
    vmem = pl.BlockSpec(memory_space=pltpu.VMEM)
    return pl.pallas_call(
        unit_kernel,
        in_specs=[pl.BlockSpec(memory_space=pltpu.SMEM)]
        + [pl.BlockSpec(memory_space=pl.ANY)] * len(ring_img)
        + [pl.BlockSpec(memory_space=pltpu.HBM)],
        out_specs=[vmem] * 6,
        out_shape=[
            jax.ShapeDtypeStruct((images, rows, width), bf16),
            jax.ShapeDtypeStruct((images, rows, width), bf16),
            jax.ShapeDtypeStruct((texts, rows, width), bf16),
            jax.ShapeDtypeStruct((images, rows, 1), f32),
            jax.ShapeDtypeStruct((texts, rows, 1), f32),
            jax.ShapeDtypeStruct((images, width), f32),
        ],
        scratch_shapes=[
            pltpu.VMEM((len(ring_img), 2, rows, width), bf16),
            pltpu.VMEM((texts, rows, width), bf16),
            pltpu.SemaphoreType.DMA((2, len(ring_img))),
        ],
        compiler_params=pltpu.CompilerParams(vmem_limit_bytes=24 * 2**20),
        cost_estimate=pl.CostEstimate(
            flops=4 * (images + texts) * rows * width,
            bytes_accessed=6 * (images + texts) * rows * width,
            transcendentals=0,
        ),
        name="gather_units",
    )(where, *ring_img, raw_txt)


def direction_kernel(turn, left_ref, inv_ref, low_hbm, raw_hbm, out_hbm, low, raw, out, *rest):
    in_sems, out_sems = rest[-2:]
    blocks, rows, _ = raw.shape
    part = blocks // 4
    loads = [
        pltpu.make_async_copy(low_hbm, low, in_sems.at[0]),
        pltpu.make_async_copy(raw_hbm, raw, in_sems.at[1]),
    ]
    for load in loads:
        load.start()
    left = left_ref
    if turn:
        left = rest[0]
        left[...] = left_ref[...].T
    for load in loads:
        load.wait()
    stores = []
    for k in range(4):
        total = jnp.dot(
            left[pl.ds(k * part * rows, part * rows), :], low[...], preferred_element_type=f32
        )
        for m in range(part):
            unit = raw[k * part + m].astype(f32) * inv_ref[k * part + m]
            piece = project(total[m * rows : (m + 1) * rows], unit)
            out[k * part + m] = piece.astype(out.dtype)
        piece = pl.ds(k * part, part)
        stores.append(pltpu.make_async_copy(out.at[piece], out_hbm.at[piece], out_sems.at[k]))
        stores[-1].start()
    for store in stores:
        store.wait()


def directions(turn, dlogit, low, raw, inv, kind):
    vmem = pl.BlockSpec(memory_space=pltpu.VMEM)
    hbm = pl.BlockSpec(memory_space=pltpu.HBM)
    turned = [pltpu.VMEM(dlogit.shape[::-1], bf16)] if turn else []
    return pl.pallas_call(
        functools.partial(direction_kernel, turn),
        in_specs=[vmem] * 2 + [pl.BlockSpec(memory_space=pl.ANY)] * 2,
        out_specs=hbm,
        out_shape=jax.ShapeDtypeStruct(raw.shape, kind),
        scratch_shapes=[
            pltpu.VMEM(low.shape, bf16),
            pltpu.VMEM(raw.shape, bf16),
            pltpu.VMEM(raw.shape, kind),
        ]
        + turned
        + [pltpu.SemaphoreType.DMA((2,)), pltpu.SemaphoreType.DMA((4,))],
        compiler_params=pltpu.CompilerParams(vmem_limit_bytes=60 * 2**20),
        cost_estimate=pl.CostEstimate(
            flops=2 * dlogit.size * low.shape[1], bytes_accessed=4 * raw.size, transcendentals=0
        ),
        name="directions",
    )(dlogit, inv, low, raw)


def project(partial, unit):
    return partial - unit * jnp.sum(unit * partial, axis=1, keepdims=True)


def head_kernel(
    seq, spots_ref, temper_ref, cached_ref, raw_ref, mean_ref, act_a, act_b, weights_hbm,
    mixed_ref, grad_ref, out_t, proj, act_rows, sems,
):
    hidden, emb = out_t.shape[1], proj.shape[1]
    loads = [
        pltpu.make_async_copy(weights_hbm.at[:, pl.ds(2 * hidden, emb)], proj, sems.at[0]),
        pltpu.make_async_copy(weights_hbm.at[:, pl.ds(hidden, hidden)], out_t, sems.at[1]),
    ]
    for load in loads:
        load.start()
    images = cached_ref.shape[0]
    half = images // 2
    for k in range(images):
        row = act_a[k] if k < half else act_b[k - half]
        act_rows[pl.ds(spots_ref[k], 1), :] = row
    act_low = act_rows[...].astype(bf16)
    cached_dir = temper_ref[0] * jnp.sum(cached_ref[...], axis=0)
    unit, inverse = unit_rows(raw_ref[...])
    grad_low = (inverse * project(cached_dir, unit)).astype(bf16)
    loads[0].wait()
    dpool_low = contract_cols(grad_low, proj[...]).astype(bf16)
    loads[1].wait()
    act_grad = jnp.dot(dpool_low, out_t[...], preferred_element_type=f32) / seq
    for k in range(images):
        grad_ref[k] = act_grad[k : k + 1]
    own = lax.broadcasted_iota(jnp.int32, (images, 1), 0) == spots_ref[images]
    pool_part = contract_cols(act_low, out_t[...]) + jnp.where(own, mean_ref[...], 0.0)
    pool_high = pool_part.astype(bf16).astype(f32)
    pool_rest = pool_part - pool_high
    dpool = dpool_low.astype(f32)
    chips = mixed_ref.shape[0]
    rows = pool_part.shape[1] // chips
    first = hidden + emb
    for k in range(chips):
        mixed_ref[k, :, 0:hidden] = act_low
        mixed_ref[k, :, hidden:first] = grad_low
        for m, array in enumerate((dpool, pool_high, pool_rest)):
            start = first + 128 * m
            mixed_ref[k, :, start : start + rows] = array[:, k * rows : (k + 1) * rows].astype(bf16)


def head(seq, spots, temper, cached, raw, mean, act_a, act_b, weights, chips):
    images, _, emb = cached.shape
    hidden = act_a.shape[2]
    width = weights.shape[0]
    smem = pl.BlockSpec(memory_space=pltpu.SMEM)
    vmem = pl.BlockSpec(memory_space=pltpu.VMEM)
    return pl.pallas_call(
        functools.partial(head_kernel, seq),
        in_specs=[smem] * 2 + [vmem] * 5 + [pl.BlockSpec(memory_space=pltpu.HBM)],
        out_specs=[vmem] * 2,
        out_shape=[
            jax.ShapeDtypeStruct((chips, images, hidden + emb + 3 * 128), bf16),
            jax.ShapeDtypeStruct((images, 1, hidden), f32),
        ],
        scratch_shapes=[
            pltpu.VMEM((width, hidden), bf16),
            pltpu.VMEM((width, emb), bf16),
            pltpu.VMEM((images, hidden), f32),
            pltpu.SemaphoreType.DMA((2,)),
        ],
        compiler_params=pltpu.CompilerParams(vmem_limit_bytes=60 * 2**20),
        cost_estimate=pl.CostEstimate(
            flops=4 * images * width * (hidden + emb),
            bytes_accessed=2 * width * (hidden + emb),
            transcendentals=0,
        ),
        name="head",
    )(spots, temper, cached, raw, mean, act_a, act_b, weights)


def on_device(image_emb, text_emb, pairs, logit_scale, tokens, norm_gain, w_in, w_out, proj):
    dp_size = lax.axis_size("dp")
    cols = lax.axis_size("col")
    ring = cols // 2
    hidden = w_in.shape[1]
    rows_d = w_in.shape[0]
    _, seq, width = tokens.shape
    temper = logit_scale[0]
    own_col = lax.axis_index("col")
    place, side = own_col // 2, own_col % 2
    core = lax.axis_index("dp") % 2
    swap = [(i, i ^ 1) for i in range(dp_size)]
    chips = [list(range(0, dp_size, 2)), list(range(1, dp_size, 2))]

    far_dp = dp_size // 2
    both = ("dp", "col")
    twin = [((d + far_dp) % dp_size) * cols + (c ^ 1) for d in range(dp_size) for c in range(cols)]
    row_groups = [
        [((d + far_dp * (c % 2)) % dp_size) * cols + c for c in range(cols)] for d in range(dp_size)
    ]

    def across(piece):
        return lax.ppermute(piece, both, list(enumerate(twin)))

    def share_rows(piece):
        return share(piece, both, row_groups)

    def along(piece, hop):
        return lax.ppermute(piece, "col", [(i, (i - 2 * hop) % cols) for i in range(cols)])

    hops = (0, 1, 3, 2)
    shard = jnp.concatenate((w_in, w_out.T, proj), axis=1)
    own_tok = tokens[0]
    raw_txt = lax.all_gather(text_emb, "dp", axis=0, tiled=True)
    weights = lax.all_gather(shard, "dp", axis=0, tiled=True)
    other_img = across(image_emb)
    other_pairs = across(pairs)
    near = [along(own_tok, hop) for hop in (1, 3)]
    own_tok, other_img, other_pairs, near = lax.optimization_barrier(
        (own_tok, other_img, other_pairs, near)
    )
    pair_img = jnp.stack((image_emb, other_img))
    ring_img = [pair_img] + [along(pair_img, hop) for hop in hops[1:]]
    other_tok = across(own_tok)
    ring_img, raw_txt, own_tok = lax.optimization_barrier((ring_img, raw_txt, own_tok))
    facing = along(own_tok, 2)
    own_rows, emb = image_emb.shape
    raw_txt = raw_txt.reshape(dp_size, own_rows, emb)
    where = [((place + hop) % ring) * 2 + flag for hop in hops for flag in (side, 1 - side)]
    order = jnp.stack([where[k] for k in (0, 2, 4, 1, 6, 3, 5, 7)]).astype(jnp.int32)
    where = jnp.stack(where + [core]).astype(jnp.int32)
    raw_img, img_low, txt_low, img_inv, txt_inv, cached_raw = gather_units(where, ring_img, raw_txt)
    img_low = img_low.reshape(-1, emb)
    txt_low = txt_low.reshape(-1, emb)
    logits = temper * contract_cols(img_low, txt_low)
    txt_count = txt_low.shape[0]
    col_base = own_col * txt_count
    group_pairs = jnp.where(
        (jnp.arange(cols, dtype=jnp.int32) % 2 == side)[:, None],
        pairs.reshape(cols, own_rows),
        other_pairs.reshape(cols, own_rows),
    ).reshape(-1)
    matches = (
        group_pairs[:, None] == col_base + jnp.arange(txt_count, dtype=jnp.int32)[None, :]
    ).astype(f32)
    row_top = jnp.max(logits, axis=1)
    row_mass = jnp.sum(jnp.exp(logits - row_top[:, None]), axis=1)
    col_top = jnp.max(logits, axis=0)
    col_mass = jnp.sum(jnp.exp(logits - col_top[None, :]), axis=0)
    row_top, row_mass, facing = lax.optimization_barrier((row_top, row_mass, facing))
    row_stats = share_rows(jnp.stack((row_top, row_mass)))
    row_stats, other_tok = lax.optimization_barrier((row_stats, other_tok))
    far = [along(other_tok, hop) for hop in (1, 3)]
    col_stats = share(jnp.stack((col_top, col_mass)), "dp")
    gain = norm_gain[None, :]
    first = encode([[own_tok], [near[0]], [near[1]], [other_tok]], gain, weights, hidden)

    def lse(stats):
        peak = jnp.max(stats[:, 0], axis=0)
        return peak + jnp.log(jnp.sum(stats[:, 1] * jnp.exp(stats[:, 0] - peak), axis=0))

    row_stats, col_stats, far, other_tok = lax.optimization_barrier(
        (row_stats, col_stats, far, other_tok)
    )
    far_facing = along(other_tok, 2)
    row_lse = lse(row_stats)
    col_lse = lse(col_stats)
    dlogit = (
        0.5 * (jnp.exp(logits - row_lse[:, None]) + jnp.exp(logits - col_lse[None, :])) - matches
    ).astype(bf16)

    cached_part = jnp.dot(
        dlogit.reshape(cols, own_rows, txt_count)[:, 0], txt_low, preferred_element_type=f32
    )
    txt_part = directions(True, dlogit, img_low, raw_txt, txt_inv, f32)
    txt_sum = lax.psum_scatter(txt_part.reshape(-1, emb), "dp", scatter_dimension=0, tiled=True)
    second = encode([[facing], [far[0]], [far[1]], [far_facing]], gain, weights, hidden)
    own_mean = jnp.mean(own_tok.astype(f32), axis=0, keepdims=True)
    spots = jnp.concatenate((order, own_col[None]))
    cached_all = share_rows(cached_part)
    img_part = directions(False, dlogit, txt_low, raw_img, img_inv, bf16)
    cached_all, first, second, own_mean, img_part = lax.optimization_barrier(
        (cached_all, first, second, own_mean, img_part)
    )
    img_pairs = img_part.reshape(ring, 2, own_rows, emb)

    def to_place(hop):
        return lax.dynamic_index_in_dim(img_pairs, (place + hop) % ring, 0, keepdims=False)

    img_terms = [along(to_place(ring - hop), hop) for hop in hops[1:]]
    _, own_img_inv = unit_rows(image_emb)
    _, own_txt_inv = unit_rows(text_emb)

    mixed, act_grad = head(
        seq, spots, logit_scale, cached_all, cached_raw, own_mean, first[4], second[4], weights, dp_size
    )
    keep, send = weigh(
        core.astype(jnp.int32)[None],
        order,
        (first[:4], second[:4]),
        act_grad,
        rows_d,
    )
    mixed = lax.all_to_all(mixed, "dp", 0, 0, tiled=True)
    send, mixed, img_terms = lax.optimization_barrier((send, mixed, img_terms))
    received = lax.ppermute(send, "dp", swap)
    mixed = mixed.reshape(-1, mixed.shape[2])
    act_all, low_all = mixed[:, :hidden], mixed[:, hidden : hidden + emb]
    dpool_all, pool_high, pool_rest = (
        mixed[:, hidden + emb + 128 * k : hidden + emb + 128 * k + rows_d] for k in range(3)
    )
    grad_w_out = contract_rows(act_all, dpool_all)
    pool_all = pool_high.astype(f32) + pool_rest.astype(f32)
    pair_sum = to_place(0).astype(f32) + sum(term.astype(f32) for term in img_terms)
    received, pair_sum, pool_all, grad_w_out = lax.optimization_barrier(
        (received, pair_sum, pool_all, grad_w_out)
    )
    for partner in (lambda x: x ^ 1, lambda x: ring - 1 - x):
        hop = [(c, partner(c // 2) * 2 + c % 2) for c in range(cols)]
        pool_all += lax.ppermute(pool_all, "col", hop)
    half = pool_all.shape[0] // 2
    turned = jnp.concatenate((pool_all[half:], pool_all[:half]))
    pool_all += lax.ppermute(turned, "col", [(c, c ^ 1) for c in range(cols)])
    pool_all = pool_all.astype(bf16)
    grad_proj = contract_rows(pool_all, low_all)
    chip_sum = (keep + received.astype(f32)).astype(bf16)
    in_sum = lax.all_to_all(chip_sum, "dp", 0, 0, axis_index_groups=chips, tiled=True)
    kept = jnp.where(side == 0, pair_sum[0], pair_sum[1])
    away = jnp.where(side == 0, pair_sum[1], pair_sum[0])
    img_sum = kept + across(away.astype(bf16)).astype(f32)
    image_grad = own_img_inv * temper * img_sum
    in_sum, txt_sum = lax.optimization_barrier((in_sum, txt_sum))
    text_grad = own_txt_inv * temper * txt_sum
    grad_w_in = jnp.sum(in_sum.astype(f32), axis=0)
    return (image_grad, text_grad, grad_w_in, grad_w_out, grad_proj)


def solution(mesh):
    in_specs = (
        P(("dp", "col"), None),
        P(("col", "dp"), None),
        P("dp"),
        P(),
        P(("dp", "col"), None, None),
        P(),
        P("dp", "col"),
        P("col", "dp"),
        P("dp", None),
    )
    out_specs = (
        P(("dp", "col"), None),
        P(("col", "dp"), None),
        P("dp", "col"),
        P("col", "dp"),
        P("dp", None),
    )
    return jax.shard_map(
        on_device, mesh=mesh, in_specs=in_specs, out_specs=out_specs, check_vma=False
    )
```

```python
import functools

import jax
import jax.numpy as jnp
from jax import lax
from jax.experimental import pallas as pl
from jax.experimental.pallas import tpu as pltpu
from jax.sharding import PartitionSpec as P

epsilon = 1e-06
inv_root_two_pi = 0.3989422804014327
root_half = 0.7071067811865476
bf16 = jnp.bfloat16
f32 = jnp.float32


def unit_rows(raw):
    values = raw.astype(f32)
    inverse = lax.rsqrt(jnp.sum(values * values, axis=-1, keepdims=True) + epsilon)
    return (values * inverse, inverse)


def contract_rows(left, right):
    return lax.dot_general(left, right, (((0,), (0,)), ((), ())), preferred_element_type=f32)


def contract_cols(left, right):
    return lax.dot_general(left, right, (((1,), (1,)), ((), ())), preferred_element_type=f32)


def share(piece, axis, groups=None):
    count = len(groups[0]) if groups else lax.axis_size(axis)
    copies = jnp.broadcast_to(piece[None], (count,) + piece.shape)
    return lax.all_to_all(copies, axis, 0, 0, axis_index_groups=groups, tiled=True)


def encode_kernel(cuts, *refs):
    images = len(cuts)
    pieces = 1 + max(cut[0] for image in cuts for cut in image)
    toks, refs = refs[:pieces], refs[pieces:]
    gain_ref, win_ref, main_ref, last_ref, slope_ref, slope_last_ref, act_ref, slots, sems = refs
    step = pl.program_id(0)

    def copies(index):
        slot = index % 2
        return [
            pltpu.make_async_copy(
                toks[piece], slots.at[slot, :, pl.ds(start, size)], sems.at[slot, k]
            )
            for k, (piece, start, size) in enumerate(cuts[index])
        ]

    def each(index, act):
        for k in range(images):

            @pl.when(index == k)
            def _():
                for copy in copies(k):
                    act(copy)

    @pl.when(step == 0)
    def _():
        each(step, lambda copy: copy.start())

    @pl.when(step + 1 < images)
    def _():
        each(step + 1, lambda copy: copy.start())

    each(step, lambda copy: copy.wait())
    slot = lax.rem(step, 2)
    floats = slots[slot].astype(f32)
    seq = floats.shape[0]
    center = jnp.mean(floats, axis=1, keepdims=True)
    shifted = floats - center
    spread = jnp.mean(shifted * shifted, axis=1, keepdims=True)
    wide = shifted * lax.rsqrt(spread + epsilon) * gain_ref[...]
    normed = wide.astype(bf16)
    main_ref[...] = normed[: seq - 1].T
    last_ref[0] = normed[seq - 1 :]
    pre = jnp.dot(normed, win_ref[...], preferred_element_type=f32)
    half = 0.5 * (1.0 + lax.erf(pre * root_half))
    act_ref[0] = jnp.sum(pre * half, axis=0, keepdims=True) * (1.0 / seq)
    slope = half + pre * jnp.exp(-0.5 * pre * pre) * inv_root_two_pi
    slope_ref[0] = slope[: seq - 1]
    slope_last_ref[0] = slope[seq - 1 :]


def encode(tokens, gain, weights, hidden):
    seq, width = tokens[0][0].shape[0], sum(piece.shape[1] for piece in tokens[0])
    images = len(tokens)
    pieces, cuts = [], []
    for image in tokens:
        ends = [sum(piece.shape[1] for piece in image[:k]) for k in range(len(image))]
        cuts.append(
            [(len(pieces) + k, end, piece.shape[1]) for k, (end, piece) in enumerate(zip(ends, image))]
        )
        pieces += image
    return pl.pallas_call(
        functools.partial(encode_kernel, cuts),
        grid=(images,),
        in_specs=[pl.BlockSpec(memory_space=pltpu.HBM)] * len(pieces)
        + [
            pl.BlockSpec((1, width), lambda i: (0, 0)),
            pl.BlockSpec((width, hidden), lambda i: (0, 0)),
        ],
        out_specs=[
            pl.BlockSpec((width, seq - 1), lambda i: (0, i)),
            pl.BlockSpec((1, 1, width), lambda i: (i, 0, 0)),
            pl.BlockSpec((1, seq - 1, hidden), lambda i: (i, 0, 0)),
            pl.BlockSpec((1, 1, hidden), lambda i: (i, 0, 0)),
            pl.BlockSpec((1, 1, hidden), lambda i: (i, 0, 0)),
        ],
        out_shape=[
            jax.ShapeDtypeStruct((width, images * (seq - 1)), bf16),
            jax.ShapeDtypeStruct((images, 1, width), bf16),
            jax.ShapeDtypeStruct((images, seq - 1, hidden), f32),
            jax.ShapeDtypeStruct((images, 1, hidden), f32),
            jax.ShapeDtypeStruct((images, 1, hidden), f32),
        ],
        scratch_shapes=[
            pltpu.VMEM((2, seq, width), bf16),
            pltpu.SemaphoreType.DMA((2, 2)),
        ],
        compiler_params=pltpu.CompilerParams(vmem_limit_bytes=60 * 2**20),
        cost_estimate=pl.CostEstimate(
            flops=2 * images * seq * width * hidden,
            bytes_accessed=images * seq * (4 * width + 4 * hidden),
            transcendentals=images * seq * hidden * 2,
        ),
        name="encode",
    )(*pieces, gain, weights)


def weigh_kernel(core_ref, order_ref, *refs):
    grad_ref, keep_ref, send_ref, pre_grad, pre_last, last_rows, last_term, total = refs[-8:]
    sets = (refs[0:4], refs[4:8])
    images, tokens, _ = sets[0][2].shape

    @pl.when(pl.program_id(0) == 0)
    def _():
        for k, (_, last_ref, slope_ref, slope_last_ref) in enumerate(sets):
            for i in range(images):
                row = grad_ref[order_ref[k * images + i]]
                pre_grad[k, pl.ds(i * tokens, tokens), :] = (slope_ref[i] * row).astype(bf16)
                pre_last[pl.ds(k * images + i, 1), :] = slope_last_ref[i] * row
                last_rows[pl.ds(k * images + i, 1), :] = last_ref[i].astype(f32)
        last_term[...] = contract_rows(last_rows[...].astype(bf16), pre_last[...].astype(bf16))

    chunk = total.shape[0]
    value = last_term[pl.ds(pl.multiple_of(pl.program_id(0) * chunk, 8), chunk), :]
    for k, (main_ref, _, _, _) in enumerate(sets):
        value += jnp.dot(main_ref[...], pre_grad[k], preferred_element_type=f32)
    total[...] = value
    core = core_ref[0]
    pairs, rows, _ = keep_ref.shape
    for pair in range(pairs):
        mine = pl.multiple_of((2 * pair + core) * rows, 8)
        other = pl.multiple_of((2 * pair + 1 - core) * rows, 8)
        keep_ref[pair] = total[pl.ds(mine, rows), :]
        send_ref[pair] = total[pl.ds(other, rows), :].astype(bf16)


def weigh(core, order, sets, act_grad, rows):
    main, _, slope, _ = sets[0]
    images, tokens, hidden = slope.shape
    width = main.shape[0]
    chunk = 4 * rows
    steps = width // chunk
    set_specs = [
        pl.BlockSpec((chunk, images * tokens), lambda i: (i, 0)),
        pl.BlockSpec((images, 1, width), lambda i: (0, 0, 0)),
        pl.BlockSpec((images, tokens, hidden), lambda i: (0, 0, 0)),
        pl.BlockSpec((images, 1, hidden), lambda i: (0, 0, 0)),
    ]
    operands = []
    for main, last, slope, slope_last in sets:
        operands += [main, last, slope, slope_last]
    return pl.pallas_call(
        weigh_kernel,
        grid=(steps,),
        in_specs=[pl.BlockSpec(memory_space=pltpu.SMEM)] * 2
        + set_specs * len(sets)
        + [pl.BlockSpec(act_grad.shape, lambda i: (0, 0, 0))],
        out_specs=[
            pl.BlockSpec((2, rows, hidden), lambda i: (i, 0, 0)),
            pl.BlockSpec((2, rows, hidden), lambda i: (i, 0, 0)),
        ],
        out_shape=[
            jax.ShapeDtypeStruct((2 * steps, rows, hidden), f32),
            jax.ShapeDtypeStruct((2 * steps, rows, hidden), bf16),
        ],
        scratch_shapes=[
            pltpu.VMEM((len(sets), images * tokens, hidden), bf16),
            pltpu.VMEM((len(sets) * images, hidden), f32),
            pltpu.VMEM((len(sets) * images, width), f32),
            pltpu.VMEM((width, hidden), f32),
            pltpu.VMEM((chunk, hidden), f32),
        ],
        compiler_params=pltpu.CompilerParams(vmem_limit_bytes=60 * 2**20),
        cost_estimate=pl.CostEstimate(
            flops=4 * images * tokens * width * hidden,
            bytes_accessed=2 * images * tokens * (2 * width + 4 * hidden),
            transcendentals=0,
        ),
        name="weigh",
    )(core, order, *operands, act_grad)


def unit_kernel(where_ref, *refs):
    pieces = refs[:-10]
    txt_hbm, raw_img, low_img, low_txt, inv_img, inv_txt, first_rows, halves, raw_txt, sems = refs[-10:]
    blocks = raw_txt.shape[0]
    part = blocks // len(pieces)
    img_loads, txt_loads = [], []
    for hop, piece in enumerate(pieces):
        chunk = pl.ds(hop * part, part)
        img_loads.append(pltpu.make_async_copy(piece, halves.at[hop], sems.at[0, hop]))
        txt_loads.append(
            pltpu.make_async_copy(txt_hbm.at[chunk], raw_txt.at[chunk], sems.at[1, hop])
        )
    for load in img_loads + txt_loads:
        load.start()
    for hop, load in enumerate(img_loads):
        load.wait()
        for flag in range(2):
            spot = where_ref[2 * hop + flag]
            values = halves[hop, flag]
            unit, inverse = unit_rows(values)
            raw_img[spot] = values
            first_rows[pl.ds(spot, 1), :] = values[0:1].astype(f32)
            low_img[spot] = unit.astype(bf16)
            inv_img[spot] = inverse
    for hop, load in enumerate(txt_loads):
        load.wait()
        for k in range(hop * part, hop * part + part):
            unit, inverse = unit_rows(raw_txt[k])
            low_txt[k] = unit.astype(bf16)
            inv_txt[k] = inverse


def gather_units(where, ring_img, raw_txt):
    texts, rows, width = raw_txt.shape
    images = 2 * len(ring_img)
    vmem = pl.BlockSpec(memory_space=pltpu.VMEM)
    return pl.pallas_call(
        unit_kernel,
        in_specs=[pl.BlockSpec(memory_space=pltpu.SMEM)]
        + [pl.BlockSpec(memory_space=pltpu.HBM)] * len(ring_img)
        + [pl.BlockSpec(memory_space=pltpu.HBM)],
        out_specs=[vmem] * 6,
        out_shape=[
            jax.ShapeDtypeStruct((images, rows, width), bf16),
            jax.ShapeDtypeStruct((images, rows, width), bf16),
            jax.ShapeDtypeStruct((texts, rows, width), bf16),
            jax.ShapeDtypeStruct((images, rows, 1), f32),
            jax.ShapeDtypeStruct((texts, rows, 1), f32),
            jax.ShapeDtypeStruct((images, width), f32),
        ],
        scratch_shapes=[
            pltpu.VMEM((len(ring_img), 2, rows, width), bf16),
            pltpu.VMEM((texts, rows, width), bf16),
            pltpu.SemaphoreType.DMA((2, len(ring_img))),
        ],
        compiler_params=pltpu.CompilerParams(vmem_limit_bytes=24 * 2**20),
        cost_estimate=pl.CostEstimate(
            flops=4 * (images + texts) * rows * width,
            bytes_accessed=6 * (images + texts) * rows * width,
            transcendentals=0,
        ),
        name="gather_units",
    )(where, *ring_img, raw_txt)


def direction_kernel(turn, left_ref, inv_ref, low_hbm, raw_hbm, out_hbm, low, raw, out, *rest):
    in_sems, out_sems = rest[-2:]
    blocks, rows, _ = raw.shape
    part = blocks // 4
    loads = [
        pltpu.make_async_copy(low_hbm, low, in_sems.at[0]),
        pltpu.make_async_copy(raw_hbm, raw, in_sems.at[1]),
    ]
    for load in loads:
        load.start()
    left = left_ref
    if turn:
        left = rest[0]
        left[...] = left_ref[...].T
    for load in loads:
        load.wait()
    stores = []
    for k in range(4):
        total = jnp.dot(
            left[pl.ds(k * part * rows, part * rows), :], low[...], preferred_element_type=f32
        )
        for m in range(part):
            unit = raw[k * part + m].astype(f32) * inv_ref[k * part + m]
            piece = project(total[m * rows : (m + 1) * rows], unit)
            out[k * part + m] = piece.astype(out.dtype)
        piece = pl.ds(k * part, part)
        stores.append(pltpu.make_async_copy(out.at[piece], out_hbm.at[piece], out_sems.at[k]))
        stores[-1].start()
    for store in stores:
        store.wait()


def directions(turn, dlogit, low, raw, inv, kind):
    vmem = pl.BlockSpec(memory_space=pltpu.VMEM)
    hbm = pl.BlockSpec(memory_space=pltpu.HBM)
    turned = [pltpu.VMEM(dlogit.shape[::-1], bf16)] if turn else []
    return pl.pallas_call(
        functools.partial(direction_kernel, turn),
        in_specs=[vmem] * 2 + [hbm] * 2,
        out_specs=hbm,
        out_shape=jax.ShapeDtypeStruct(raw.shape, kind),
        scratch_shapes=[
            pltpu.VMEM(low.shape, bf16),
            pltpu.VMEM(raw.shape, bf16),
            pltpu.VMEM(raw.shape, kind),
        ]
        + turned
        + [pltpu.SemaphoreType.DMA((2,)), pltpu.SemaphoreType.DMA((4,))],
        compiler_params=pltpu.CompilerParams(vmem_limit_bytes=60 * 2**20),
        cost_estimate=pl.CostEstimate(
            flops=2 * dlogit.size * low.shape[1], bytes_accessed=4 * raw.size, transcendentals=0
        ),
        name="directions",
    )(dlogit, inv, low, raw)


def project(partial, unit):
    return partial - unit * jnp.sum(unit * partial, axis=1, keepdims=True)


def head_kernel(
    seq, spots_ref, temper_ref, cached_ref, raw_ref, mean_ref, act_a, act_b, weights_hbm,
    mixed_ref, grad_ref, out_t, proj, act_rows, sems,
):
    hidden, emb = out_t.shape[1], proj.shape[1]
    loads = [
        pltpu.make_async_copy(weights_hbm.at[:, pl.ds(2 * hidden, emb)], proj, sems.at[0]),
        pltpu.make_async_copy(weights_hbm.at[:, pl.ds(hidden, hidden)], out_t, sems.at[1]),
    ]
    for load in loads:
        load.start()
    images = cached_ref.shape[0]
    half = images // 2
    for k in range(images):
        row = act_a[k] if k < half else act_b[k - half]
        act_rows[pl.ds(spots_ref[k], 1), :] = row
    act_low = act_rows[...].astype(bf16)
    cached_dir = temper_ref[0] * jnp.sum(cached_ref[...], axis=0)
    unit, inverse = unit_rows(raw_ref[...])
    grad_low = (inverse * project(cached_dir, unit)).astype(bf16)
    loads[0].wait()
    dpool_low = contract_cols(grad_low, proj[...]).astype(bf16)
    loads[1].wait()
    act_grad = jnp.dot(dpool_low, out_t[...], preferred_element_type=f32) / seq
    for k in range(images):
        grad_ref[k] = act_grad[k : k + 1]
    own = lax.broadcasted_iota(jnp.int32, (images, 1), 0) == spots_ref[images]
    pool_part = contract_cols(act_low, out_t[...]) + jnp.where(own, mean_ref[...], 0.0)
    pool_high = pool_part.astype(bf16).astype(f32)
    pool_rest = pool_part - pool_high
    dpool = dpool_low.astype(f32)
    chips = mixed_ref.shape[0]
    rows = pool_part.shape[1] // chips
    first = hidden + emb
    for k in range(chips):
        mixed_ref[k, :, 0:hidden] = act_low
        mixed_ref[k, :, hidden:first] = grad_low
        for m, array in enumerate((dpool, pool_high, pool_rest)):
            start = first + 128 * m
            mixed_ref[k, :, start : start + rows] = array[:, k * rows : (k + 1) * rows].astype(bf16)


def head(seq, spots, temper, cached, raw, mean, act_a, act_b, weights, chips):
    images, _, emb = cached.shape
    hidden = act_a.shape[2]
    width = weights.shape[0]
    smem = pl.BlockSpec(memory_space=pltpu.SMEM)
    vmem = pl.BlockSpec(memory_space=pltpu.VMEM)
    return pl.pallas_call(
        functools.partial(head_kernel, seq),
        in_specs=[smem] * 2 + [vmem] * 5 + [pl.BlockSpec(memory_space=pltpu.HBM)],
        out_specs=[vmem] * 2,
        out_shape=[
            jax.ShapeDtypeStruct((chips, images, hidden + emb + 3 * 128), bf16),
            jax.ShapeDtypeStruct((images, 1, hidden), f32),
        ],
        scratch_shapes=[
            pltpu.VMEM((width, hidden), bf16),
            pltpu.VMEM((width, emb), bf16),
            pltpu.VMEM((images, hidden), f32),
            pltpu.SemaphoreType.DMA((2,)),
        ],
        compiler_params=pltpu.CompilerParams(vmem_limit_bytes=60 * 2**20),
        cost_estimate=pl.CostEstimate(
            flops=4 * images * width * (hidden + emb),
            bytes_accessed=2 * width * (hidden + emb),
            transcendentals=0,
        ),
        name="head",
    )(spots, temper, cached, raw, mean, act_a, act_b, weights)


def on_device(image_emb, text_emb, pairs, logit_scale, tokens, norm_gain, w_in, w_out, proj):
    dp_size = lax.axis_size("dp")
    cols = lax.axis_size("col")
    ring = cols // 2
    hidden = w_in.shape[1]
    rows_d = w_in.shape[0]
    _, seq, width = tokens.shape
    temper = logit_scale[0]
    own_col = lax.axis_index("col")
    place, side = own_col // 2, own_col % 2
    core = lax.axis_index("dp") % 2
    swap = [(i, i ^ 1) for i in range(dp_size)]
    chips = [list(range(0, dp_size, 2)), list(range(1, dp_size, 2))]

    far_dp = dp_size // 2
    both = ("dp", "col")
    twin = [((d + far_dp) % dp_size) * cols + (c ^ 1) for d in range(dp_size) for c in range(cols)]
    row_groups = [
        [((d + far_dp * (c % 2)) % dp_size) * cols + c for c in range(cols)] for d in range(dp_size)
    ]

    def across(piece):
        return lax.ppermute(piece, both, list(enumerate(twin)))

    def share_rows(piece):
        return share(piece, both, row_groups)

    def along(piece, hop):
        return lax.ppermute(piece, "col", [(i, (i - 2 * hop) % cols) for i in range(cols)])

    hops = (0, 1, 3, 2)
    shard = jnp.concatenate((w_in, w_out.T, proj), axis=1)
    own_tok = tokens[0]
    raw_txt = lax.all_gather(text_emb, "dp", axis=0, tiled=True)
    weights = lax.all_gather(shard, "dp", axis=0, tiled=True)
    other_img = across(image_emb)
    other_pairs = across(pairs)
    near = [along(own_tok, hop) for hop in (1, 3)]
    own_tok, other_img, other_pairs, near = lax.optimization_barrier(
        (own_tok, other_img, other_pairs, near)
    )
    pair_img = jnp.stack((image_emb, other_img))
    ring_img = [pair_img] + [along(pair_img, hop) for hop in hops[1:]]
    other_tok = across(own_tok)
    ring_img, raw_txt, own_tok = lax.optimization_barrier((ring_img, raw_txt, own_tok))
    facing = along(own_tok, 2)
    own_rows, emb = image_emb.shape
    raw_txt = raw_txt.reshape(dp_size, own_rows, emb)
    where = [((place + hop) % ring) * 2 + flag for hop in hops for flag in (side, 1 - side)]
    order = jnp.stack([where[k] for k in (0, 2, 4, 1, 6, 3, 5, 7)]).astype(jnp.int32)
    where = jnp.stack(where + [core]).astype(jnp.int32)
    spots = jnp.concatenate((order, own_col[None]))
    own_mean = jnp.mean(own_tok.astype(f32), axis=0, keepdims=True)
    raw_img, img_low, txt_low, img_inv, txt_inv, cached_raw = gather_units(where, ring_img, raw_txt)
    img_low = img_low.reshape(-1, emb)
    txt_low = txt_low.reshape(-1, emb)
    logits = temper * contract_cols(img_low, txt_low)
    txt_count = txt_low.shape[0]
    col_base = own_col * txt_count
    group_pairs = jnp.where(
        (jnp.arange(cols, dtype=jnp.int32) % 2 == side)[:, None],
        pairs.reshape(cols, own_rows),
        other_pairs.reshape(cols, own_rows),
    ).reshape(-1)
    matches = (
        group_pairs[:, None] == col_base + jnp.arange(txt_count, dtype=jnp.int32)[None, :]
    ).astype(f32)
    row_top = jnp.max(logits, axis=1)
    row_mass = jnp.sum(jnp.exp(logits - row_top[:, None]), axis=1)
    col_top = jnp.max(logits, axis=0)
    col_mass = jnp.sum(jnp.exp(logits - col_top[None, :]), axis=0)
    row_top, row_mass, facing, order, spots, own_mean = lax.optimization_barrier(
        (row_top, row_mass, facing, order, spots, own_mean)
    )
    row_stats = share_rows(jnp.stack((row_top, row_mass)))
    row_stats, other_tok, facing = lax.optimization_barrier((row_stats, other_tok, facing))
    far = [along(other_tok, hop) for hop in (1, 3)]
    far_facing = across(facing)
    col_stats = share(jnp.stack((col_top, col_mass)), "dp")
    gain = norm_gain[None, :]
    first = encode([[own_tok], [near[0]], [near[1]], [other_tok]], gain, weights, hidden)

    def lse(stats):
        peak = jnp.max(stats[:, 0], axis=0)
        return peak + jnp.log(jnp.sum(stats[:, 1] * jnp.exp(stats[:, 0] - peak), axis=0))

    row_stats, col_stats, far, far_facing, first = lax.optimization_barrier(
        (row_stats, col_stats, far, far_facing, first)
    )
    row_lse = lse(row_stats)
    col_lse = lse(col_stats)
    dlogit = (
        0.5 * (jnp.exp(logits - row_lse[:, None]) + jnp.exp(logits - col_lse[None, :])) - matches
    ).astype(bf16)

    cached_part = jnp.dot(
        dlogit.reshape(cols, own_rows, txt_count)[:, 0], txt_low, preferred_element_type=f32
    )
    txt_part = directions(True, dlogit, img_low, raw_txt, txt_inv, f32)
    txt_sum = lax.psum_scatter(txt_part.reshape(-1, emb), "dp", scatter_dimension=0, tiled=True)
    second = encode([[facing], [far[0]], [far[1]], [far_facing]], gain, weights, hidden)
    cached_all = share_rows(cached_part)
    img_part = directions(False, dlogit, txt_low, raw_img, img_inv, bf16)
    cached_all, second, img_part = lax.optimization_barrier((cached_all, second, img_part))
    img_pairs = img_part.reshape(ring, 2, own_rows, emb)

    def to_place(hop):
        return lax.dynamic_index_in_dim(img_pairs, (place + hop) % ring, 0, keepdims=False)

    img_terms = [along(to_place(ring - hop), hop) for hop in hops[1:]]
    _, own_img_inv = unit_rows(image_emb)
    _, own_txt_inv = unit_rows(text_emb)

    mixed, act_grad = head(
        seq, spots, logit_scale, cached_all, cached_raw, own_mean, first[4], second[4], weights, dp_size
    )
    keep, send = weigh(
        core.astype(jnp.int32)[None],
        order,
        (first[:4], second[:4]),
        act_grad,
        rows_d,
    )
    mixed = lax.all_to_all(mixed, "dp", 0, 0, tiled=True)
    send, mixed, img_terms = lax.optimization_barrier((send, mixed, img_terms))
    received = lax.ppermute(send, "dp", swap)
    mixed = mixed.reshape(-1, mixed.shape[2])
    act_all, low_all = mixed[:, :hidden], mixed[:, hidden : hidden + emb]
    dpool_all, pool_high, pool_rest = (
        mixed[:, hidden + emb + 128 * k : hidden + emb + 128 * k + rows_d] for k in range(3)
    )
    grad_w_out = contract_rows(act_all, dpool_all)
    pool_all = pool_high.astype(f32) + pool_rest.astype(f32)
    pair_sum = to_place(0).astype(f32) + sum(term.astype(f32) for term in img_terms)
    received, pair_sum, pool_all, grad_w_out = lax.optimization_barrier(
        (received, pair_sum, pool_all, grad_w_out)
    )
    for partner in (lambda x: x ^ 1, lambda x: ring - 1 - x):
        hop = [(c, partner(c // 2) * 2 + c % 2) for c in range(cols)]
        pool_all += lax.ppermute(pool_all, "col", hop)
    half = pool_all.shape[0] // 2
    turned = jnp.concatenate((pool_all[half:], pool_all[:half]))
    pool_all += lax.ppermute(turned, "col", [(c, c ^ 1) for c in range(cols)])
    pool_all = pool_all.astype(bf16)
    grad_proj = contract_rows(pool_all, low_all)
    chip_sum = (keep + received.astype(f32)).astype(bf16)
    in_sum = lax.all_to_all(chip_sum, "dp", 0, 0, axis_index_groups=chips, tiled=True)
    kept = jnp.where(side == 0, pair_sum[0], pair_sum[1])
    away = jnp.where(side == 0, pair_sum[1], pair_sum[0])
    img_sum = kept + across(away.astype(bf16)).astype(f32)
    image_grad = own_img_inv * temper * img_sum
    in_sum, txt_sum = lax.optimization_barrier((in_sum, txt_sum))
    text_grad = own_txt_inv * temper * txt_sum
    grad_w_in = jnp.sum(in_sum.astype(f32), axis=0)
    return (image_grad, text_grad, grad_w_in, grad_w_out, grad_proj)


def solution(mesh):
    in_specs = (
        P(("dp", "col"), None),
        P(("col", "dp"), None),
        P("dp"),
        P(),
        P(("dp", "col"), None, None),
        P(),
        P("dp", "col"),
        P("col", "dp"),
        P("dp", None),
    )
    out_specs = (
        P(("dp", "col"), None),
        P(("col", "dp"), None),
        P("dp", "col"),
        P("col", "dp"),
        P("dp", None),
    )
    return jax.shard_map(
        on_device, mesh=mesh, in_specs=in_specs, out_specs=out_specs, check_vma=False
    )
```

```python
import functools

import jax
import jax.numpy as jnp
from jax import lax
from jax.experimental import pallas as pl
from jax.experimental.pallas import tpu as pltpu
from jax.sharding import PartitionSpec as P

epsilon = 1e-06
inv_root_two_pi = 0.3989422804014327
root_half = 0.7071067811865476
bf16 = jnp.bfloat16
f32 = jnp.float32


def unit_rows(raw):
    values = raw.astype(f32)
    inverse = lax.rsqrt(jnp.sum(values * values, axis=-1, keepdims=True) + epsilon)
    return (values * inverse, inverse)


def contract_rows(left, right):
    return lax.dot_general(left, right, (((0,), (0,)), ((), ())), preferred_element_type=f32)


def contract_cols(left, right):
    return lax.dot_general(left, right, (((1,), (1,)), ((), ())), preferred_element_type=f32)


def share(piece, axis, groups=None):
    count = len(groups[0]) if groups else lax.axis_size(axis)
    copies = jnp.broadcast_to(piece[None], (count,) + piece.shape)
    return lax.all_to_all(copies, axis, 0, 0, axis_index_groups=groups, tiled=True)


def encode_kernel(cuts, *refs):
    images = len(cuts)
    pieces = 1 + max(cut[0] for image in cuts for cut in image)
    toks, refs = refs[:pieces], refs[pieces:]
    gain_ref, win_ref, main_ref, last_ref, slope_ref, slope_last_ref, act_ref, slots, sems = refs
    step = pl.program_id(0)

    def copies(index):
        slot = index % 2
        return [
            pltpu.make_async_copy(
                toks[piece], slots.at[slot, :, pl.ds(start, size)], sems.at[slot, k]
            )
            for k, (piece, start, size) in enumerate(cuts[index])
        ]

    def each(index, act):
        for k in range(images):

            @pl.when(index == k)
            def _():
                for copy in copies(k):
                    act(copy)

    @pl.when(step == 0)
    def _():
        each(step, lambda copy: copy.start())

    @pl.when(step + 1 < images)
    def _():
        each(step + 1, lambda copy: copy.start())

    each(step, lambda copy: copy.wait())
    slot = lax.rem(step, 2)
    floats = slots[slot].astype(f32)
    seq = floats.shape[0]
    center = jnp.mean(floats, axis=1, keepdims=True)
    shifted = floats - center
    spread = jnp.mean(shifted * shifted, axis=1, keepdims=True)
    wide = shifted * lax.rsqrt(spread + epsilon) * gain_ref[...]
    normed = wide.astype(bf16)
    main_ref[...] = normed[: seq - 1].T
    last_ref[0] = normed[seq - 1 :]
    pre = jnp.dot(normed, win_ref[...], preferred_element_type=f32)
    half = 0.5 * (1.0 + lax.erf(pre * root_half))
    act_ref[0] = jnp.sum(pre * half, axis=0, keepdims=True) * (1.0 / seq)
    slope = half + pre * jnp.exp(-0.5 * pre * pre) * inv_root_two_pi
    slope_ref[0] = slope[: seq - 1].astype(bf16)
    slope_last_ref[0] = slope[seq - 1 :]


def encode(tokens, gain, weights, hidden):
    seq, width = tokens[0][0].shape[0], sum(piece.shape[1] for piece in tokens[0])
    images = len(tokens)
    pieces, cuts = [], []
    for image in tokens:
        ends = [sum(piece.shape[1] for piece in image[:k]) for k in range(len(image))]
        cuts.append(
            [(len(pieces) + k, end, piece.shape[1]) for k, (end, piece) in enumerate(zip(ends, image))]
        )
        pieces += image
    return pl.pallas_call(
        functools.partial(encode_kernel, cuts),
        grid=(images,),
        in_specs=[pl.BlockSpec(memory_space=pltpu.HBM)] * len(pieces)
        + [
            pl.BlockSpec((1, width), lambda i: (0, 0)),
            pl.BlockSpec((width, hidden), lambda i: (0, 0)),
        ],
        out_specs=[
            pl.BlockSpec((width, seq - 1), lambda i: (0, i)),
            pl.BlockSpec((1, 1, width), lambda i: (i, 0, 0)),
            pl.BlockSpec((1, seq - 1, hidden), lambda i: (i, 0, 0)),
            pl.BlockSpec((1, 1, hidden), lambda i: (i, 0, 0)),
            pl.BlockSpec((1, 1, hidden), lambda i: (i, 0, 0)),
        ],
        out_shape=[
            jax.ShapeDtypeStruct((width, images * (seq - 1)), bf16),
            jax.ShapeDtypeStruct((images, 1, width), bf16),
            jax.ShapeDtypeStruct((images, seq - 1, hidden), bf16),
            jax.ShapeDtypeStruct((images, 1, hidden), f32),
            jax.ShapeDtypeStruct((images, 1, hidden), f32),
        ],
        scratch_shapes=[
            pltpu.VMEM((2, seq, width), bf16),
            pltpu.SemaphoreType.DMA((2, 2)),
        ],
        compiler_params=pltpu.CompilerParams(vmem_limit_bytes=60 * 2**20),
        cost_estimate=pl.CostEstimate(
            flops=2 * images * seq * width * hidden,
            bytes_accessed=images * seq * (4 * width + 4 * hidden),
            transcendentals=images * seq * hidden * 2,
        ),
        name="encode",
    )(*pieces, gain, weights)


def weigh_kernel(core_ref, order_ref, *refs):
    grad_ref, keep_ref, send_ref, pre_grad, pre_last, last_rows, last_term, total = refs[-8:]
    sets = (refs[0:4], refs[4:8])
    images, tokens, _ = sets[0][2].shape

    @pl.when(pl.program_id(0) == 0)
    def _():
        for k, (_, last_ref, slope_ref, slope_last_ref) in enumerate(sets):
            for i in range(images):
                row = grad_ref[order_ref[k * images + i]]
                pre_grad[k, pl.ds(i * tokens, tokens), :] = (slope_ref[i].astype(f32) * row).astype(bf16)
                pre_last[pl.ds(k * images + i, 1), :] = slope_last_ref[i] * row
                last_rows[pl.ds(k * images + i, 1), :] = last_ref[i].astype(f32)
        last_term[...] = contract_rows(last_rows[...].astype(bf16), pre_last[...].astype(bf16))

    chunk = total.shape[0]
    value = last_term[pl.ds(pl.multiple_of(pl.program_id(0) * chunk, 8), chunk), :]
    for k, (main_ref, _, _, _) in enumerate(sets):
        value += jnp.dot(main_ref[...], pre_grad[k], preferred_element_type=f32)
    total[...] = value
    core = core_ref[0]
    pairs, rows, _ = keep_ref.shape
    for pair in range(pairs):
        mine = pl.multiple_of((2 * pair + core) * rows, 8)
        other = pl.multiple_of((2 * pair + 1 - core) * rows, 8)
        keep_ref[pair] = total[pl.ds(mine, rows), :]
        send_ref[pair] = total[pl.ds(other, rows), :].astype(bf16)


def weigh(core, order, sets, act_grad, rows):
    main, _, slope, _ = sets[0]
    images, tokens, hidden = slope.shape
    width = main.shape[0]
    chunk = 4 * rows
    steps = width // chunk
    set_specs = [
        pl.BlockSpec((chunk, images * tokens), lambda i: (i, 0)),
        pl.BlockSpec((images, 1, width), lambda i: (0, 0, 0)),
        pl.BlockSpec((images, tokens, hidden), lambda i: (0, 0, 0)),
        pl.BlockSpec((images, 1, hidden), lambda i: (0, 0, 0)),
    ]
    operands = []
    for main, last, slope, slope_last in sets:
        operands += [main, last, slope, slope_last]
    return pl.pallas_call(
        weigh_kernel,
        grid=(steps,),
        in_specs=[pl.BlockSpec(memory_space=pltpu.SMEM)] * 2
        + set_specs * len(sets)
        + [pl.BlockSpec(act_grad.shape, lambda i: (0, 0, 0))],
        out_specs=[
            pl.BlockSpec((2, rows, hidden), lambda i: (i, 0, 0)),
            pl.BlockSpec((2, rows, hidden), lambda i: (i, 0, 0)),
        ],
        out_shape=[
            jax.ShapeDtypeStruct((2 * steps, rows, hidden), f32),
            jax.ShapeDtypeStruct((2 * steps, rows, hidden), bf16),
        ],
        scratch_shapes=[
            pltpu.VMEM((len(sets), images * tokens, hidden), bf16),
            pltpu.VMEM((len(sets) * images, hidden), f32),
            pltpu.VMEM((len(sets) * images, width), f32),
            pltpu.VMEM((width, hidden), f32),
            pltpu.VMEM((chunk, hidden), f32),
        ],
        compiler_params=pltpu.CompilerParams(vmem_limit_bytes=60 * 2**20),
        cost_estimate=pl.CostEstimate(
            flops=4 * images * tokens * width * hidden,
            bytes_accessed=2 * images * tokens * (2 * width + 4 * hidden),
            transcendentals=0,
        ),
        name="weigh",
    )(core, order, *operands, act_grad)


def unit_kernel(where_ref, *refs):
    pieces = refs[:-10]
    txt_hbm, raw_img, low_img, low_txt, inv_img, inv_txt, first_rows, halves, raw_txt, sems = refs[-10:]
    blocks = raw_txt.shape[0]
    part = blocks // len(pieces)
    img_loads, txt_loads = [], []
    for hop, piece in enumerate(pieces):
        chunk = pl.ds(hop * part, part)
        img_loads.append(pltpu.make_async_copy(piece, halves.at[hop], sems.at[0, hop]))
        txt_loads.append(
            pltpu.make_async_copy(txt_hbm.at[chunk], raw_txt.at[chunk], sems.at[1, hop])
        )
    for load in img_loads + txt_loads:
        load.start()
    for hop, load in enumerate(img_loads):
        load.wait()
        for flag in range(2):
            spot = where_ref[2 * hop + flag]
            values = halves[hop, flag]
            unit, inverse = unit_rows(values)
            raw_img[spot] = values
            first_rows[pl.ds(spot, 1), :] = values[0:1].astype(f32)
            low_img[spot] = unit.astype(bf16)
            inv_img[spot] = inverse
    for hop, load in enumerate(txt_loads):
        load.wait()
        for k in range(hop * part, hop * part + part):
            unit, inverse = unit_rows(raw_txt[k])
            low_txt[k] = unit.astype(bf16)
            inv_txt[k] = inverse


def gather_units(where, ring_img, raw_txt):
    texts, rows, width = raw_txt.shape
    images = 2 * len(ring_img)
    vmem = pl.BlockSpec(memory_space=pltpu.VMEM)
    return pl.pallas_call(
        unit_kernel,
        in_specs=[pl.BlockSpec(memory_space=pltpu.SMEM)]
        + [pl.BlockSpec(memory_space=pltpu.HBM)] * len(ring_img)
        + [pl.BlockSpec(memory_space=pltpu.HBM)],
        out_specs=[vmem] * 6,
        out_shape=[
            jax.ShapeDtypeStruct((images, rows, width), bf16),
            jax.ShapeDtypeStruct((images, rows, width), bf16),
            jax.ShapeDtypeStruct((texts, rows, width), bf16),
            jax.ShapeDtypeStruct((images, rows, 1), f32),
            jax.ShapeDtypeStruct((texts, rows, 1), f32),
            jax.ShapeDtypeStruct((images, width), f32),
        ],
        scratch_shapes=[
            pltpu.VMEM((len(ring_img), 2, rows, width), bf16),
            pltpu.VMEM((texts, rows, width), bf16),
            pltpu.SemaphoreType.DMA((2, len(ring_img))),
        ],
        compiler_params=pltpu.CompilerParams(vmem_limit_bytes=60 * 2**20),
        cost_estimate=pl.CostEstimate(
            flops=4 * (images + texts) * rows * width,
            bytes_accessed=6 * (images + texts) * rows * width,
            transcendentals=0,
        ),
        name="gather_units",
    )(where, *ring_img, raw_txt)


def direction_kernel(turn, left_ref, inv_ref, low_hbm, raw_hbm, out_hbm, low, raw, out, *rest):
    in_sems, out_sems = rest[-2:]
    blocks, rows, _ = raw.shape
    part = blocks // 4
    loads = [
        pltpu.make_async_copy(low_hbm, low, in_sems.at[0]),
        pltpu.make_async_copy(raw_hbm, raw, in_sems.at[1]),
    ]
    for load in loads:
        load.start()
    left = left_ref
    if turn:
        left = rest[0]
        left[...] = left_ref[...].T
    for load in loads:
        load.wait()
    stores = []
    for k in range(4):
        total = jnp.dot(
            left[pl.ds(k * part * rows, part * rows), :], low[...], preferred_element_type=f32
        )
        for m in range(part):
            unit = raw[k * part + m].astype(f32) * inv_ref[k * part + m]
            piece = project(total[m * rows : (m + 1) * rows], unit)
            out[k * part + m] = piece.astype(out.dtype)
        piece = pl.ds(k * part, part)
        stores.append(pltpu.make_async_copy(out.at[piece], out_hbm.at[piece], out_sems.at[k]))
        stores[-1].start()
    for store in stores:
        store.wait()


def directions(turn, dlogit, low, raw, inv, kind):
    vmem = pl.BlockSpec(memory_space=pltpu.VMEM)
    hbm = pl.BlockSpec(memory_space=pltpu.HBM)
    turned = [pltpu.VMEM(dlogit.shape[::-1], bf16)] if turn else []
    return pl.pallas_call(
        functools.partial(direction_kernel, turn),
        in_specs=[vmem] * 2 + [hbm] * 2,
        out_specs=hbm,
        out_shape=jax.ShapeDtypeStruct(raw.shape, kind),
        scratch_shapes=[
            pltpu.VMEM(low.shape, bf16),
            pltpu.VMEM(raw.shape, bf16),
            pltpu.VMEM(raw.shape, kind),
        ]
        + turned
        + [pltpu.SemaphoreType.DMA((2,)), pltpu.SemaphoreType.DMA((4,))],
        compiler_params=pltpu.CompilerParams(vmem_limit_bytes=60 * 2**20),
        cost_estimate=pl.CostEstimate(
            flops=2 * dlogit.size * low.shape[1], bytes_accessed=4 * raw.size, transcendentals=0
        ),
        name="directions",
    )(dlogit, inv, low, raw)


def project(partial, unit):
    return partial - unit * jnp.sum(unit * partial, axis=1, keepdims=True)


def head_kernel(
    seq, spots_ref, temper_ref, cached_ref, raw_ref, mean_ref, act_a, act_b, weights_hbm,
    mixed_ref, grad_ref, out_t, proj, act_rows, sems,
):
    hidden, emb = out_t.shape[1], proj.shape[1]
    loads = [
        pltpu.make_async_copy(weights_hbm.at[:, pl.ds(2 * hidden, emb)], proj, sems.at[0]),
        pltpu.make_async_copy(weights_hbm.at[:, pl.ds(hidden, hidden)], out_t, sems.at[1]),
    ]
    for load in loads:
        load.start()
    images = cached_ref.shape[0]
    half = images // 2
    for k in range(images):
        row = act_a[k] if k < half else act_b[k - half]
        act_rows[pl.ds(spots_ref[k], 1), :] = row
    act_low = act_rows[...].astype(bf16)
    cached_dir = temper_ref[0] * jnp.sum(cached_ref[...], axis=0)
    unit, inverse = unit_rows(raw_ref[...])
    grad_low = (inverse * project(cached_dir, unit)).astype(bf16)
    loads[0].wait()
    dpool_low = contract_cols(grad_low, proj[...]).astype(bf16)
    loads[1].wait()
    act_grad = jnp.dot(dpool_low, out_t[...], preferred_element_type=f32) / seq
    for k in range(images):
        grad_ref[k] = act_grad[k : k + 1]
    own = lax.broadcasted_iota(jnp.int32, (images, 1), 0) == spots_ref[images]
    pool_part = contract_cols(act_low, out_t[...]) + jnp.where(own, mean_ref[...], 0.0)
    pool_high = pool_part.astype(bf16).astype(f32)
    pool_rest = pool_part - pool_high
    dpool = dpool_low.astype(f32)
    chips = mixed_ref.shape[0]
    rows = pool_part.shape[1] // chips
    first = hidden + emb
    for k in range(chips):
        mixed_ref[k, :, 0:hidden] = act_low
        mixed_ref[k, :, hidden:first] = grad_low
        for m, array in enumerate((dpool, pool_high, pool_rest)):
            start = first + 128 * m
            mixed_ref[k, :, start : start + rows] = array[:, k * rows : (k + 1) * rows].astype(bf16)


def head(seq, spots, temper, cached, raw, mean, act_a, act_b, weights, chips):
    images, _, emb = cached.shape
    hidden = act_a.shape[2]
    width = weights.shape[0]
    smem = pl.BlockSpec(memory_space=pltpu.SMEM)
    vmem = pl.BlockSpec(memory_space=pltpu.VMEM)
    return pl.pallas_call(
        functools.partial(head_kernel, seq),
        in_specs=[smem] * 2 + [vmem] * 5 + [pl.BlockSpec(memory_space=pltpu.HBM)],
        out_specs=[vmem] * 2,
        out_shape=[
            jax.ShapeDtypeStruct((chips, images, hidden + emb + 3 * 128), bf16),
            jax.ShapeDtypeStruct((images, 1, hidden), f32),
        ],
        scratch_shapes=[
            pltpu.VMEM((width, hidden), bf16),
            pltpu.VMEM((width, emb), bf16),
            pltpu.VMEM((images, hidden), f32),
            pltpu.SemaphoreType.DMA((2,)),
        ],
        compiler_params=pltpu.CompilerParams(vmem_limit_bytes=60 * 2**20),
        cost_estimate=pl.CostEstimate(
            flops=4 * images * width * (hidden + emb),
            bytes_accessed=2 * width * (hidden + emb),
            transcendentals=0,
        ),
        name="head",
    )(spots, temper, cached, raw, mean, act_a, act_b, weights)


def on_device(image_emb, text_emb, pairs, logit_scale, tokens, norm_gain, w_in, w_out, proj):
    dp_size = lax.axis_size("dp")
    cols = lax.axis_size("col")
    ring = cols // 2
    hidden = w_in.shape[1]
    rows_d = w_in.shape[0]
    _, seq, width = tokens.shape
    temper = logit_scale[0]
    own_col = lax.axis_index("col")
    place, side = own_col // 2, own_col % 2
    core = lax.axis_index("dp") % 2
    swap = [(i, i ^ 1) for i in range(dp_size)]
    chips = [list(range(0, dp_size, 2)), list(range(1, dp_size, 2))]

    far_dp = dp_size // 2
    both = ("dp", "col")
    twin = [((d + far_dp) % dp_size) * cols + (c ^ 1) for d in range(dp_size) for c in range(cols)]
    row_groups = [
        [((d + far_dp * (c % 2)) % dp_size) * cols + c for c in range(cols)] for d in range(dp_size)
    ]

    def across(piece):
        return lax.ppermute(piece, both, list(enumerate(twin)))

    def share_rows(piece):
        return share(piece, both, row_groups)

    def along(piece, hop):
        return lax.ppermute(piece, "col", [(i, (i - 2 * hop) % cols) for i in range(cols)])

    hops = (0, 1, 3, 2)
    shard = jnp.concatenate((w_in, w_out.T, proj), axis=1)
    own_tok = tokens[0]
    raw_txt = lax.all_gather(text_emb, "dp", axis=0, tiled=True)
    weights = lax.all_gather(shard, "dp", axis=0, tiled=True)
    other_img = across(image_emb)
    other_pairs = across(pairs)
    near = [along(own_tok, hop) for hop in (1, 3)]
    own_tok, other_img, other_pairs, near = lax.optimization_barrier(
        (own_tok, other_img, other_pairs, near)
    )
    pair_img = jnp.stack((image_emb, other_img))
    ring_img = [pair_img] + [along(pair_img, hop) for hop in hops[1:]]
    other_tok = across(own_tok)
    ring_img, raw_txt, own_tok = lax.optimization_barrier((ring_img, raw_txt, own_tok))
    facing = along(own_tok, 2)
    own_rows, emb = image_emb.shape
    raw_txt = raw_txt.reshape(dp_size, own_rows, emb)
    where = [((place + hop) % ring) * 2 + flag for hop in hops for flag in (side, 1 - side)]
    order = jnp.stack([where[k] for k in (0, 2, 4, 1, 6, 3, 5, 7)]).astype(jnp.int32)
    where = jnp.stack(where + [core]).astype(jnp.int32)
    spots = jnp.concatenate((order, own_col[None]))
    own_mean = jnp.mean(own_tok.astype(f32), axis=0, keepdims=True)
    raw_img, img_low, txt_low, img_inv, txt_inv, cached_raw = gather_units(where, ring_img, raw_txt)
    img_low = img_low.reshape(-1, emb)
    txt_low = txt_low.reshape(-1, emb)
    logits = temper * contract_cols(img_low, txt_low)
    txt_count = txt_low.shape[0]
    col_base = own_col * txt_count
    group_pairs = jnp.where(
        (jnp.arange(cols, dtype=jnp.int32) % 2 == side)[:, None],
        pairs.reshape(cols, own_rows),
        other_pairs.reshape(cols, own_rows),
    ).reshape(-1)
    matches = (
        group_pairs[:, None] == col_base + jnp.arange(txt_count, dtype=jnp.int32)[None, :]
    ).astype(f32)
    row_top = jnp.max(logits, axis=1)
    row_mass = jnp.sum(jnp.exp(logits - row_top[:, None]), axis=1)
    col_top = jnp.max(logits, axis=0)
    col_mass = jnp.sum(jnp.exp(logits - col_top[None, :]), axis=0)
    row_top, row_mass, order, spots, own_mean = lax.optimization_barrier(
        (row_top, row_mass, order, spots, own_mean)
    )
    row_stats = share_rows(jnp.stack((row_top, row_mass)))
    row_stats, other_tok, facing = lax.optimization_barrier((row_stats, other_tok, facing))
    far = [along(other_tok, hop) for hop in (1, 3)]
    far_facing = across(facing)
    col_stats = share(jnp.stack((col_top, col_mass)), "dp")
    gain = norm_gain[None, :]
    first = encode([[own_tok], [near[0]], [near[1]], [other_tok]], gain, weights, hidden)

    def lse(stats):
        peak = jnp.max(stats[:, 0], axis=0)
        return peak + jnp.log(jnp.sum(stats[:, 1] * jnp.exp(stats[:, 0] - peak), axis=0))

    row_stats, col_stats, far = lax.optimization_barrier((row_stats, col_stats, far))
    row_lse = lse(row_stats)
    col_lse = lse(col_stats)
    dlogit = (
        0.5 * (jnp.exp(logits - row_lse[:, None]) + jnp.exp(logits - col_lse[None, :])) - matches
    ).astype(bf16)

    cached_part = jnp.dot(
        dlogit.reshape(cols, own_rows, txt_count)[:, 0], txt_low, preferred_element_type=f32
    )
    txt_part = directions(True, dlogit, img_low, raw_txt, txt_inv, f32)
    txt_sum = lax.psum_scatter(txt_part.reshape(-1, emb), "dp", scatter_dimension=0, tiled=True)
    second = encode([[facing], [far[0]], [far[1]], [far_facing]], gain, weights, hidden)
    cached_all = share_rows(cached_part)
    img_part = directions(False, dlogit, txt_low, raw_img, img_inv, bf16)
    cached_all, first, second, img_part = lax.optimization_barrier(
        (cached_all, first, second, img_part)
    )
    img_pairs = img_part.reshape(ring, 2, own_rows, emb)

    def to_place(hop):
        return lax.dynamic_index_in_dim(img_pairs, (place + hop) % ring, 0, keepdims=False)

    img_terms = [along(to_place(ring - hop), hop) for hop in hops[1:]]
    _, own_img_inv = unit_rows(image_emb)
    _, own_txt_inv = unit_rows(text_emb)

    mixed, act_grad = head(
        seq, spots, logit_scale, cached_all, cached_raw, own_mean, first[4], second[4], weights, dp_size
    )
    keep, send = weigh(
        core.astype(jnp.int32)[None],
        order,
        (first[:4], second[:4]),
        act_grad,
        rows_d,
    )
    mixed = lax.all_to_all(mixed, "dp", 0, 0, tiled=True)
    send, mixed, img_terms = lax.optimization_barrier((send, mixed, img_terms))
    received = lax.ppermute(send, "dp", swap)
    mixed = mixed.reshape(-1, mixed.shape[2])
    act_all, low_all = mixed[:, :hidden], mixed[:, hidden : hidden + emb]
    dpool_all, pool_high, pool_rest = (
        mixed[:, hidden + emb + 128 * k : hidden + emb + 128 * k + rows_d] for k in range(3)
    )
    grad_w_out = contract_rows(act_all, dpool_all)
    pool_all = pool_high.astype(f32) + pool_rest.astype(f32)
    pair_sum = to_place(0).astype(f32) + sum(term.astype(f32) for term in img_terms)
    received, pair_sum, pool_all, grad_w_out = lax.optimization_barrier(
        (received, pair_sum, pool_all, grad_w_out)
    )
    for partner in (lambda x: x ^ 1, lambda x: ring - 1 - x):
        hop = [(c, partner(c // 2) * 2 + c % 2) for c in range(cols)]
        pool_all += lax.ppermute(pool_all, "col", hop)
    half = pool_all.shape[0] // 2
    turned = jnp.concatenate((pool_all[half:], pool_all[:half]))
    pool_all += lax.ppermute(turned, "col", [(c, c ^ 1) for c in range(cols)])
    pool_all = pool_all.astype(bf16)
    grad_proj = contract_rows(pool_all, low_all)
    chip_sum = (keep + received.astype(f32)).astype(bf16)
    in_sum = lax.all_to_all(chip_sum, "dp", 0, 0, axis_index_groups=chips, tiled=True)
    kept = jnp.where(side == 0, pair_sum[0], pair_sum[1])
    away = jnp.where(side == 0, pair_sum[1], pair_sum[0])
    img_sum = kept + across(away.astype(bf16)).astype(f32)
    image_grad = own_img_inv * temper * img_sum
    in_sum, txt_sum = lax.optimization_barrier((in_sum, txt_sum))
    text_grad = own_txt_inv * temper * txt_sum
    grad_w_in = jnp.sum(in_sum.astype(f32), axis=0)
    return (image_grad, text_grad, grad_w_in, grad_w_out, grad_proj)


def solution(mesh):
    in_specs = (
        P(("dp", "col"), None),
        P(("col", "dp"), None),
        P("dp"),
        P(),
        P(("dp", "col"), None, None),
        P(),
        P("dp", "col"),
        P("col", "dp"),
        P("dp", None),
    )
    out_specs = (
        P(("dp", "col"), None),
        P(("col", "dp"), None),
        P("dp", "col"),
        P("col", "dp"),
        P("dp", None),
    )
    return jax.shard_map(
        on_device, mesh=mesh, in_specs=in_specs, out_specs=out_specs, check_vma=False
    )
```

```python
import functools

import jax
import jax.numpy as jnp
from jax import lax
from jax.experimental import pallas as pl
from jax.experimental.pallas import tpu as pltpu
from jax.sharding import PartitionSpec as P

epsilon = 1e-06
inv_root_two_pi = 0.3989422804014327
root_half = 0.7071067811865476
bf16 = jnp.bfloat16
f32 = jnp.float32


def unit_rows(raw):
    values = raw.astype(f32)
    inverse = lax.rsqrt(jnp.sum(values * values, axis=-1, keepdims=True) + epsilon)
    return (values * inverse, inverse)


def contract_rows(left, right):
    return lax.dot_general(left, right, (((0,), (0,)), ((), ())), preferred_element_type=f32)


def contract_cols(left, right):
    return lax.dot_general(left, right, (((1,), (1,)), ((), ())), preferred_element_type=f32)


def share(piece, axis, groups=None):
    count = len(groups[0]) if groups else lax.axis_size(axis)
    copies = jnp.broadcast_to(piece[None], (count,) + piece.shape)
    return lax.all_to_all(copies, axis, 0, 0, axis_index_groups=groups, tiled=True)


def encode_kernel(cuts, *refs):
    images = len(cuts)
    pieces = 1 + max(cut[0] for image in cuts for cut in image)
    toks, refs = refs[:pieces], refs[pieces:]
    gain_ref, win_ref, main_ref, last_ref, slope_ref, slope_last_ref, act_ref, slots, sems = refs
    step = pl.program_id(0)

    def copies(index):
        slot = index % 2
        return [
            pltpu.make_async_copy(
                toks[piece], slots.at[slot, :, pl.ds(start, size)], sems.at[slot, k]
            )
            for k, (piece, start, size) in enumerate(cuts[index])
        ]

    def each(index, act):
        for k in range(images):

            @pl.when(index == k)
            def _():
                for copy in copies(k):
                    act(copy)

    @pl.when(step == 0)
    def _():
        each(step, lambda copy: copy.start())

    @pl.when(step + 1 < images)
    def _():
        each(step + 1, lambda copy: copy.start())

    each(step, lambda copy: copy.wait())
    slot = lax.rem(step, 2)
    floats = slots[slot].astype(f32)
    seq = floats.shape[0]
    center = jnp.mean(floats, axis=1, keepdims=True)
    shifted = floats - center
    spread = jnp.mean(shifted * shifted, axis=1, keepdims=True)
    wide = shifted * lax.rsqrt(spread + epsilon) * gain_ref[...]
    normed = wide.astype(bf16)
    main_ref[...] = normed[: seq - 1].T
    last_ref[0] = normed[seq - 1 :]
    pre = jnp.dot(normed, win_ref[...], preferred_element_type=f32)
    half = 0.5 * (1.0 + lax.erf(pre * root_half))
    act_ref[0] = jnp.sum(pre * half, axis=0, keepdims=True) * (1.0 / seq)
    slope = half + pre * jnp.exp(-0.5 * pre * pre) * inv_root_two_pi
    slope_ref[0] = slope[: seq - 1].astype(bf16)
    slope_last_ref[0] = slope[seq - 1 :]


def encode(tokens, gain, weights, hidden):
    seq, width = tokens[0][0].shape[0], sum(piece.shape[1] for piece in tokens[0])
    images = len(tokens)
    pieces, cuts = [], []
    for image in tokens:
        ends = [sum(piece.shape[1] for piece in image[:k]) for k in range(len(image))]
        cuts.append(
            [(len(pieces) + k, end, piece.shape[1]) for k, (end, piece) in enumerate(zip(ends, image))]
        )
        pieces += image
    return pl.pallas_call(
        functools.partial(encode_kernel, cuts),
        grid=(images,),
        in_specs=[pl.BlockSpec(memory_space=pltpu.HBM)] * len(pieces)
        + [
            pl.BlockSpec((1, width), lambda i: (0, 0)),
            pl.BlockSpec((width, hidden), lambda i: (0, 0)),
        ],
        out_specs=[
            pl.BlockSpec((width, seq - 1), lambda i: (0, i)),
            pl.BlockSpec((1, 1, width), lambda i: (i, 0, 0)),
            pl.BlockSpec((1, seq - 1, hidden), lambda i: (i, 0, 0)),
            pl.BlockSpec((1, 1, hidden), lambda i: (i, 0, 0)),
            pl.BlockSpec((1, 1, hidden), lambda i: (i, 0, 0)),
        ],
        out_shape=[
            jax.ShapeDtypeStruct((width, images * (seq - 1)), bf16),
            jax.ShapeDtypeStruct((images, 1, width), bf16),
            jax.ShapeDtypeStruct((images, seq - 1, hidden), bf16),
            jax.ShapeDtypeStruct((images, 1, hidden), f32),
            jax.ShapeDtypeStruct((images, 1, hidden), f32),
        ],
        scratch_shapes=[
            pltpu.VMEM((2, seq, width), bf16),
            pltpu.SemaphoreType.DMA((2, 2)),
        ],
        compiler_params=pltpu.CompilerParams(vmem_limit_bytes=60 * 2**20),
        cost_estimate=pl.CostEstimate(
            flops=2 * images * seq * width * hidden,
            bytes_accessed=images * seq * (4 * width + 4 * hidden),
            transcendentals=images * seq * hidden * 2,
        ),
        name="encode",
    )(*pieces, gain, weights)


def weigh_kernel(core_ref, order_ref, *refs):
    grad_ref, keep_ref, send_ref, pre_grad, pre_last, last_rows, last_term, total = refs[-8:]
    sets = (refs[0:4], refs[4:8])
    images, tokens, _ = sets[0][2].shape

    @pl.when(pl.program_id(0) == 0)
    def _():
        for k, (_, last_ref, slope_ref, slope_last_ref) in enumerate(sets):
            for i in range(images):
                row = grad_ref[order_ref[k * images + i]]
                pre_grad[k, pl.ds(i * tokens, tokens), :] = (slope_ref[i].astype(f32) * row).astype(bf16)
                pre_last[pl.ds(k * images + i, 1), :] = slope_last_ref[i] * row
                last_rows[pl.ds(k * images + i, 1), :] = last_ref[i].astype(f32)
        last_term[...] = contract_rows(last_rows[...].astype(bf16), pre_last[...].astype(bf16))

    chunk = total.shape[0]
    value = last_term[pl.ds(pl.multiple_of(pl.program_id(0) * chunk, 8), chunk), :]
    for k, (main_ref, _, _, _) in enumerate(sets):
        value += jnp.dot(main_ref[...], pre_grad[k], preferred_element_type=f32)
    total[...] = value
    core = core_ref[0]
    pairs, rows, _ = keep_ref.shape
    for pair in range(pairs):
        mine = pl.multiple_of((2 * pair + core) * rows, 8)
        other = pl.multiple_of((2 * pair + 1 - core) * rows, 8)
        keep_ref[pair] = total[pl.ds(mine, rows), :]
        send_ref[pair] = total[pl.ds(other, rows), :].astype(bf16)


def weigh(core, order, sets, act_grad, rows):
    main, _, slope, _ = sets[0]
    images, tokens, hidden = slope.shape
    width = main.shape[0]
    chunk = 4 * rows
    steps = width // chunk
    set_specs = [
        pl.BlockSpec((chunk, images * tokens), lambda i: (i, 0)),
        pl.BlockSpec((images, 1, width), lambda i: (0, 0, 0)),
        pl.BlockSpec((images, tokens, hidden), lambda i: (0, 0, 0)),
        pl.BlockSpec((images, 1, hidden), lambda i: (0, 0, 0)),
    ]
    operands = []
    for main, last, slope, slope_last in sets:
        operands += [main, last, slope, slope_last]
    return pl.pallas_call(
        weigh_kernel,
        grid=(steps,),
        in_specs=[pl.BlockSpec(memory_space=pltpu.SMEM)] * 2
        + set_specs * len(sets)
        + [pl.BlockSpec(act_grad.shape, lambda i: (0, 0, 0))],
        out_specs=[
            pl.BlockSpec((2, rows, hidden), lambda i: (i, 0, 0)),
            pl.BlockSpec((2, rows, hidden), lambda i: (i, 0, 0)),
        ],
        out_shape=[
            jax.ShapeDtypeStruct((2 * steps, rows, hidden), f32),
            jax.ShapeDtypeStruct((2 * steps, rows, hidden), bf16),
        ],
        scratch_shapes=[
            pltpu.VMEM((len(sets), images * tokens, hidden), bf16),
            pltpu.VMEM((len(sets) * images, hidden), f32),
            pltpu.VMEM((len(sets) * images, width), f32),
            pltpu.VMEM((width, hidden), f32),
            pltpu.VMEM((chunk, hidden), f32),
        ],
        compiler_params=pltpu.CompilerParams(vmem_limit_bytes=60 * 2**20),
        cost_estimate=pl.CostEstimate(
            flops=4 * images * tokens * width * hidden,
            bytes_accessed=2 * images * tokens * (2 * width + 4 * hidden),
            transcendentals=0,
        ),
        name="weigh",
    )(core, order, *operands, act_grad)


def unit_kernel(where_ref, *refs):
    pieces = refs[:-10]
    txt_hbm, raw_img, low_img, low_txt, inv_img, inv_txt, first_rows, halves, raw_txt, sems = refs[-10:]
    blocks = raw_txt.shape[0]
    part = blocks // len(pieces)
    img_loads, txt_loads = [], []
    for hop, piece in enumerate(pieces):
        chunk = pl.ds(hop * part, part)
        img_loads.append(pltpu.make_async_copy(piece, halves.at[hop], sems.at[0, hop]))
        txt_loads.append(
            pltpu.make_async_copy(txt_hbm.at[chunk], raw_txt.at[chunk], sems.at[1, hop])
        )
    for load in img_loads + txt_loads:
        load.start()
    for hop, load in enumerate(img_loads):
        load.wait()
        for flag in range(2):
            spot = where_ref[2 * hop + flag]
            values = halves[hop, flag]
            unit, inverse = unit_rows(values)
            raw_img[spot] = values
            first_rows[pl.ds(spot, 1), :] = values[0:1].astype(f32)
            low_img[spot] = unit.astype(bf16)
            inv_img[spot] = inverse
    for hop, load in enumerate(txt_loads):
        load.wait()
        for k in range(hop * part, hop * part + part):
            unit, inverse = unit_rows(raw_txt[k])
            low_txt[k] = unit.astype(bf16)
            inv_txt[k] = inverse


def gather_units(where, ring_img, raw_txt):
    texts, rows, width = raw_txt.shape
    images = 2 * len(ring_img)
    vmem = pl.BlockSpec(memory_space=pltpu.VMEM)
    return pl.pallas_call(
        unit_kernel,
        in_specs=[pl.BlockSpec(memory_space=pltpu.SMEM)]
        + [pl.BlockSpec(memory_space=pltpu.HBM)] * len(ring_img)
        + [pl.BlockSpec(memory_space=pltpu.HBM)],
        out_specs=[vmem] * 6,
        out_shape=[
            jax.ShapeDtypeStruct((images, rows, width), bf16),
            jax.ShapeDtypeStruct((images, rows, width), bf16),
            jax.ShapeDtypeStruct((texts, rows, width), bf16),
            jax.ShapeDtypeStruct((images, rows, 1), f32),
            jax.ShapeDtypeStruct((texts, rows, 1), f32),
            jax.ShapeDtypeStruct((images, width), f32),
        ],
        scratch_shapes=[
            pltpu.VMEM((len(ring_img), 2, rows, width), bf16),
            pltpu.VMEM((texts, rows, width), bf16),
            pltpu.SemaphoreType.DMA((2, len(ring_img))),
        ],
        compiler_params=pltpu.CompilerParams(vmem_limit_bytes=60 * 2**20),
        cost_estimate=pl.CostEstimate(
            flops=4 * (images + texts) * rows * width,
            bytes_accessed=6 * (images + texts) * rows * width,
            transcendentals=0,
        ),
        name="gather_units",
    )(where, *ring_img, raw_txt)


def direction_kernel(
    dlogit_ref, inv_img, inv_txt, low_img_hbm, low_txt_hbm, raw_img_hbm, raw_txt_hbm,
    img_hbm, txt_hbm, low_img, low_txt, raw_img, raw_txt, img_out, txt_out, turned, in_sems, out_sems,
):
    groups, rows, _ = raw_img.shape
    many = raw_txt.shape[0]
    loads = [
        pltpu.make_async_copy(source, target, in_sems.at[k])
        for k, (source, target) in enumerate(
            (
                (low_txt_hbm, low_txt),
                (raw_img_hbm, raw_img),
                (low_img_hbm, low_img),
                (raw_txt_hbm, raw_txt),
            )
        )
    ]
    for load in loads:
        load.start()
    turned[...] = dlogit_ref[...].T
    stores = []

    def run(left, right, raw, inv, out, hbm, count):
        for k in range(4):
            part = count // 4
            total = jnp.dot(
                left[pl.ds(k * part * rows, part * rows), :], right[...], preferred_element_type=f32
            )
            for m in range(part):
                unit = raw[k * part + m].astype(f32) * inv[k * part + m]
                piece = project(total[m * rows : (m + 1) * rows], unit)
                out[k * part + m] = piece.astype(out.dtype)
            piece = pl.ds(k * part, part)
            store = pltpu.make_async_copy(out.at[piece], hbm.at[piece], out_sems.at[len(stores)])
            store.start()
            stores.append(store)

    loads[0].wait()
    loads[1].wait()
    run(dlogit_ref, low_txt, raw_img, inv_img, img_out, img_hbm, groups)
    loads[2].wait()
    loads[3].wait()
    run(turned, low_img, raw_txt, inv_txt, txt_out, txt_hbm, many)
    for store in stores:
        store.wait()


def directions(dlogit, low_img, low_txt, raw_img, raw_txt, inv_img, inv_txt):
    rows, cols = dlogit.shape
    width = low_img.shape[1]
    vmem = pl.BlockSpec(memory_space=pltpu.VMEM)
    hbm = pl.BlockSpec(memory_space=pltpu.HBM)
    return pl.pallas_call(
        direction_kernel,
        in_specs=[vmem] * 3 + [hbm] * 4,
        out_specs=[hbm] * 2,
        out_shape=[
            jax.ShapeDtypeStruct(raw_img.shape, bf16),
            jax.ShapeDtypeStruct(raw_txt.shape, f32),
        ],
        scratch_shapes=[
            pltpu.VMEM(low_img.shape, bf16),
            pltpu.VMEM(low_txt.shape, bf16),
            pltpu.VMEM(raw_img.shape, bf16),
            pltpu.VMEM(raw_txt.shape, bf16),
            pltpu.VMEM(raw_img.shape, bf16),
            pltpu.VMEM(raw_txt.shape, f32),
            pltpu.VMEM((cols, rows), bf16),
            pltpu.SemaphoreType.DMA((4,)),
            pltpu.SemaphoreType.DMA((8,)),
        ],
        compiler_params=pltpu.CompilerParams(vmem_limit_bytes=60 * 2**20),
        cost_estimate=pl.CostEstimate(
            flops=4 * rows * cols * width, bytes_accessed=10 * cols * width, transcendentals=0
        ),
        name="directions",
    )(dlogit, inv_img, inv_txt, low_img, low_txt, raw_img, raw_txt)


def project(partial, unit):
    return partial - unit * jnp.sum(unit * partial, axis=1, keepdims=True)


def head_kernel(
    seq, spots_ref, temper_ref, cached_ref, raw_ref, mean_ref, act_a, act_b, weights_hbm,
    mixed_ref, grad_ref, out_t, proj, act_rows, sems,
):
    hidden, emb = out_t.shape[1], proj.shape[1]
    loads = [
        pltpu.make_async_copy(weights_hbm.at[:, pl.ds(2 * hidden, emb)], proj, sems.at[0]),
        pltpu.make_async_copy(weights_hbm.at[:, pl.ds(hidden, hidden)], out_t, sems.at[1]),
    ]
    for load in loads:
        load.start()
    images = cached_ref.shape[0]
    half = images // 2
    for k in range(images):
        row = act_a[k] if k < half else act_b[k - half]
        act_rows[pl.ds(spots_ref[k], 1), :] = row
    act_low = act_rows[...].astype(bf16)
    cached_dir = temper_ref[0] * jnp.sum(cached_ref[...], axis=0)
    unit, inverse = unit_rows(raw_ref[...])
    grad_low = (inverse * project(cached_dir, unit)).astype(bf16)
    loads[0].wait()
    dpool_low = contract_cols(grad_low, proj[...]).astype(bf16)
    loads[1].wait()
    act_grad = jnp.dot(dpool_low, out_t[...], preferred_element_type=f32) / seq
    for k in range(images):
        grad_ref[k] = act_grad[k : k + 1]
    own = lax.broadcasted_iota(jnp.int32, (images, 1), 0) == spots_ref[images]
    pool_part = contract_cols(act_low, out_t[...]) + jnp.where(own, mean_ref[...], 0.0)
    pool_high = pool_part.astype(bf16).astype(f32)
    pool_rest = pool_part - pool_high
    dpool = dpool_low.astype(f32)
    chips = mixed_ref.shape[0]
    rows = pool_part.shape[1] // chips
    first = hidden + emb
    for k in range(chips):
        mixed_ref[k, :, 0:hidden] = act_low
        mixed_ref[k, :, hidden:first] = grad_low
        for m, array in enumerate((dpool, pool_high, pool_rest)):
            start = first + 128 * m
            mixed_ref[k, :, start : start + rows] = array[:, k * rows : (k + 1) * rows].astype(bf16)


def head(seq, spots, temper, cached, raw, mean, act_a, act_b, weights, chips):
    images, _, emb = cached.shape
    hidden = act_a.shape[2]
    width = weights.shape[0]
    smem = pl.BlockSpec(memory_space=pltpu.SMEM)
    vmem = pl.BlockSpec(memory_space=pltpu.VMEM)
    return pl.pallas_call(
        functools.partial(head_kernel, seq),
        in_specs=[smem] * 2 + [vmem] * 5 + [pl.BlockSpec(memory_space=pltpu.HBM)],
        out_specs=[vmem] * 2,
        out_shape=[
            jax.ShapeDtypeStruct((chips, images, hidden + emb + 3 * 128), bf16),
            jax.ShapeDtypeStruct((images, 1, hidden), f32),
        ],
        scratch_shapes=[
            pltpu.VMEM((width, hidden), bf16),
            pltpu.VMEM((width, emb), bf16),
            pltpu.VMEM((images, hidden), f32),
            pltpu.SemaphoreType.DMA((2,)),
        ],
        compiler_params=pltpu.CompilerParams(vmem_limit_bytes=60 * 2**20),
        cost_estimate=pl.CostEstimate(
            flops=4 * images * width * (hidden + emb),
            bytes_accessed=2 * width * (hidden + emb),
            transcendentals=0,
        ),
        name="head",
    )(spots, temper, cached, raw, mean, act_a, act_b, weights)


def on_device(image_emb, text_emb, pairs, logit_scale, tokens, norm_gain, w_in, w_out, proj):
    dp_size = lax.axis_size("dp")
    cols = lax.axis_size("col")
    ring = cols // 2
    hidden = w_in.shape[1]
    rows_d = w_in.shape[0]
    _, seq, width = tokens.shape
    temper = logit_scale[0]
    own_col = lax.axis_index("col")
    place, side = own_col // 2, own_col % 2
    core = lax.axis_index("dp") % 2
    swap = [(i, i ^ 1) for i in range(dp_size)]
    chips = [list(range(0, dp_size, 2)), list(range(1, dp_size, 2))]

    far_dp = dp_size // 2
    both = ("dp", "col")
    twin = [((d + far_dp) % dp_size) * cols + (c ^ 1) for d in range(dp_size) for c in range(cols)]
    row_groups = [
        [((d + far_dp * (c % 2)) % dp_size) * cols + c for c in range(cols)] for d in range(dp_size)
    ]

    def across(piece):
        return lax.ppermute(piece, both, list(enumerate(twin)))

    def share_rows(piece):
        return share(piece, both, row_groups)

    def along(piece, hop):
        return lax.ppermute(piece, "col", [(i, (i - 2 * hop) % cols) for i in range(cols)])

    hops = (0, 1, 3, 2)
    shard = jnp.concatenate((w_in, w_out.T, proj), axis=1)
    own_tok = tokens[0]
    raw_txt = lax.all_gather(text_emb, "dp", axis=0, tiled=True)
    weights = lax.all_gather(shard, "dp", axis=0, tiled=True)
    other_img = across(image_emb)
    other_pairs = across(pairs)
    near = [along(own_tok, hop) for hop in (1, 3)]
    own_tok, other_img, other_pairs, near = lax.optimization_barrier(
        (own_tok, other_img, other_pairs, near)
    )
    pair_img = jnp.stack((image_emb, other_img))
    ring_img = [pair_img] + [along(pair_img, hop) for hop in hops[1:]]
    other_tok = across(own_tok)
    ring_img, raw_txt, own_tok = lax.optimization_barrier((ring_img, raw_txt, own_tok))
    facing = along(own_tok, 2)
    own_rows, emb = image_emb.shape
    raw_txt = raw_txt.reshape(dp_size, own_rows, emb)
    where = [((place + hop) % ring) * 2 + flag for hop in hops for flag in (side, 1 - side)]
    order = jnp.stack([where[k] for k in (0, 2, 4, 1, 6, 3, 5, 7)]).astype(jnp.int32)
    where = jnp.stack(where + [core]).astype(jnp.int32)
    spots = jnp.concatenate((order, own_col[None]))
    own_mean = jnp.mean(own_tok.astype(f32), axis=0, keepdims=True)
    raw_img, img_low, txt_low, img_inv, txt_inv, cached_raw = gather_units(where, ring_img, raw_txt)
    img_low = img_low.reshape(-1, emb)
    txt_low = txt_low.reshape(-1, emb)
    logits = temper * contract_cols(img_low, txt_low)
    txt_count = txt_low.shape[0]
    col_base = own_col * txt_count
    group_pairs = jnp.where(
        (jnp.arange(cols, dtype=jnp.int32) % 2 == side)[:, None],
        pairs.reshape(cols, own_rows),
        other_pairs.reshape(cols, own_rows),
    ).reshape(-1)
    matches = (
        group_pairs[:, None] == col_base + jnp.arange(txt_count, dtype=jnp.int32)[None, :]
    ).astype(f32)
    row_top = jnp.max(logits, axis=1)
    row_mass = jnp.sum(jnp.exp(logits - row_top[:, None]), axis=1)
    col_top = jnp.max(logits, axis=0)
    col_mass = jnp.sum(jnp.exp(logits - col_top[None, :]), axis=0)
    row_top, row_mass, order, spots, own_mean = lax.optimization_barrier(
        (row_top, row_mass, order, spots, own_mean)
    )
    row_stats = share_rows(jnp.stack((row_top, row_mass)))
    row_stats, other_tok, facing = lax.optimization_barrier((row_stats, other_tok, facing))
    far = [along(other_tok, hop) for hop in (1, 3)]
    far_facing = across(facing)
    col_stats = share(jnp.stack((col_top, col_mass)), "dp")
    gain = norm_gain[None, :]
    first = encode([[own_tok], [near[0]], [near[1]], [other_tok]], gain, weights, hidden)

    def lse(stats):
        peak = jnp.max(stats[:, 0], axis=0)
        return peak + jnp.log(jnp.sum(stats[:, 1] * jnp.exp(stats[:, 0] - peak), axis=0))

    row_stats, col_stats, far = lax.optimization_barrier((row_stats, col_stats, far))
    row_lse = lse(row_stats)
    col_lse = lse(col_stats)
    dlogit = (
        0.5 * (jnp.exp(logits - row_lse[:, None]) + jnp.exp(logits - col_lse[None, :])) - matches
    ).astype(bf16)

    cached_part = jnp.dot(
        dlogit.reshape(cols, own_rows, txt_count)[:, 0], txt_low, preferred_element_type=f32
    )
    img_part, txt_part = directions(dlogit, img_low, txt_low, raw_img, raw_txt, img_inv, txt_inv)
    txt_sum = lax.psum_scatter(txt_part.reshape(-1, emb), "dp", scatter_dimension=0, tiled=True)
    second = encode([[facing], [far[0]], [far[1]], [far_facing]], gain, weights, hidden)
    cached_all = share_rows(cached_part)
    cached_all, first, second, img_part = lax.optimization_barrier(
        (cached_all, first, second, img_part)
    )
    img_pairs = img_part.reshape(ring, 2, own_rows, emb)

    def to_place(hop):
        return lax.dynamic_index_in_dim(img_pairs, (place + hop) % ring, 0, keepdims=False)

    img_terms = [along(to_place(ring - hop), hop) for hop in hops[1:]]
    _, own_img_inv = unit_rows(image_emb)
    _, own_txt_inv = unit_rows(text_emb)

    mixed, act_grad = head(
        seq, spots, logit_scale, cached_all, cached_raw, own_mean, first[4], second[4], weights, dp_size
    )
    keep, send = weigh(
        core.astype(jnp.int32)[None],
        order,
        (first[:4], second[:4]),
        act_grad,
        rows_d,
    )
    mixed = lax.all_to_all(mixed, "dp", 0, 0, tiled=True)
    send, mixed, img_terms = lax.optimization_barrier((send, mixed, img_terms))
    received = lax.ppermute(send, "dp", swap)
    mixed = mixed.reshape(-1, mixed.shape[2])
    act_all, low_all = mixed[:, :hidden], mixed[:, hidden : hidden + emb]
    dpool_all, pool_high, pool_rest = (
        mixed[:, hidden + emb + 128 * k : hidden + emb + 128 * k + rows_d] for k in range(3)
    )
    grad_w_out = contract_rows(act_all, dpool_all)
    pool_all = pool_high.astype(f32) + pool_rest.astype(f32)
    pair_sum = to_place(0).astype(f32) + sum(term.astype(f32) for term in img_terms)
    received, pair_sum, pool_all, grad_w_out = lax.optimization_barrier(
        (received, pair_sum, pool_all, grad_w_out)
    )
    for partner in (lambda x: x ^ 1, lambda x: ring - 1 - x):
        hop = [(c, partner(c // 2) * 2 + c % 2) for c in range(cols)]
        pool_all += lax.ppermute(pool_all, "col", hop)
    half = pool_all.shape[0] // 2
    turned = jnp.concatenate((pool_all[half:], pool_all[:half]))
    pool_all += lax.ppermute(turned, "col", [(c, c ^ 1) for c in range(cols)])
    pool_all = pool_all.astype(bf16)
    grad_proj = contract_rows(pool_all, low_all)
    chip_sum = (keep + received.astype(f32)).astype(bf16)
    in_sum = lax.all_to_all(chip_sum, "dp", 0, 0, axis_index_groups=chips, tiled=True)
    kept = jnp.where(side == 0, pair_sum[0], pair_sum[1])
    away = jnp.where(side == 0, pair_sum[1], pair_sum[0])
    img_sum = kept + across(away.astype(bf16)).astype(f32)
    image_grad = own_img_inv * temper * img_sum
    in_sum, txt_sum = lax.optimization_barrier((in_sum, txt_sum))
    text_grad = own_txt_inv * temper * txt_sum
    grad_w_in = jnp.sum(in_sum.astype(f32), axis=0)
    return (image_grad, text_grad, grad_w_in, grad_w_out, grad_proj)


def solution(mesh):
    in_specs = (
        P(("dp", "col"), None),
        P(("col", "dp"), None),
        P("dp"),
        P(),
        P(("dp", "col"), None, None),
        P(),
        P("dp", "col"),
        P("col", "dp"),
        P("dp", None),
    )
    out_specs = (
        P(("dp", "col"), None),
        P(("col", "dp"), None),
        P("dp", "col"),
        P("col", "dp"),
        P("dp", None),
    )
    return jax.shard_map(
        on_device, mesh=mesh, in_specs=in_specs, out_specs=out_specs, check_vma=False
    )
```
